256 devices in a mesh: replica: 32 (over y_hi, z, core), tensor: 8 (over x, y_lo).
Axes of the slice: x: 4, y: 4 (y_hi: 2, y_lo: 2; y = y_hi * 2 + y_lo), z: 8, core: 2. Of those that a mesh axis runs over, the one named last changes fastest.
Arguments:
- hidden: bfloat16 [4096, 4, 8192], P('replica', None, 'tensor'), may hold values from -6 to 6
- queries: bfloat16 [4096, 4, 8192], P('replica', None, 'tensor'), may hold values from -90 to 90
- key_cache_rows: bfloat16 [4096, 48, 1024], P('replica', None, 'tensor'), may hold values from -7 to 7
- value_cache_rows: bfloat16 [4096, 48, 1024], P('replica', None, 'tensor'), may hold values from -6 to 6
- lengths: int32 [4096], P('replica'), may hold values from 2 to 48, as said below
- request_adapter: int32 [4096], P('replica'), may hold values from 0 to 511, as said below
- block_first_row: int32 [1024], P('replica'), may hold values from 0 to 127, as said below
- adapter_owner_group: int32 [512], replicated, may hold values from 0 to 31, as said below
- key_value_weight: bfloat16 [8192, 2, 1024], P(None, None, 'tensor'), may hold values from -0.0625 to 0.0625
- adapter_down_weight: bfloat16 [512, 2, 32, 8192], P('replica', None, None, 'tensor'), may hold values from -0.0625 to 0.0625
- adapter_up_weight: bfloat16 [512, 2, 32, 1024], P('replica', None, None, 'tensor'), may hold values from -1 to 1
Outputs:
- fresh_kv: bfloat16 [4096, 4, 2, 1024], P('replica', None, None, 'tensor')
- attended: bfloat16 [4096, 4, 8192], P('replica', None, 'tensor')
The draws below stay inside these ranges and needn't reach their ends.
Inputs may be any that keep to these rules, and one draw needn't show every extreme that they name: `adapter_owner_group`: each replica group index holds exactly 16 adapters. block_first_row counts rows within its replica group; each group has 32 blocks in rising order starting at 0, of 1 to 7 rows each, and some block of every group has exactly 7 rows. `request_adapter`: all rows of one block name the same adapter; among the 32 blocks of one replica group at most 2 name adapters of one owner, and in every group some owner has exactly 2. `lengths`: some request of every replica group has exactly 48 live positions.
All inputs are finite; a program needn't handle non-finite values.
Results may differ from the reference program's by a relative error of at most 0.0065.
Values may be sent and summed in bfloat16 or wider, within the bound.
No kernel may reach another device: no remote copies, remote signals or barrier semaphores. Data moves between devices by JAX's collectives and lax.ppermute only.
A program may use at most 128 MiB of HBM per device.

```python
import jax
import jax.numpy as jnp
from jax import lax

MODEL_WIDTH = 8192
HD = 128
QH = 64
KVH = 8
ADAPTER_RANK = 32
APR = 16
ROWS = 128
STEPS = 4
CACHE = 48
BAVG = 4
KEY_FEATURES = 1024
ADAPTER_POOL = 512
NB = 32
CAPQ = 2
ROWS_ALL = 4096


def shared_keys(key):
    source = jax.random.fold_in(key, 501)
    return jnp.clip(jax.random.normal(source, (ROWS_ALL, CACHE, KEY_FEATURES), jnp.float32), -6.0, 6.0)


def block_layout(key):
    groups = ROWS_ALL // ROWS
    owner_key = jax.random.fold_in(key, 601)
    owners_all = (jax.random.permutation(owner_key, ADAPTER_POOL) // APR).astype(jnp.int32)
    adapter_ids = jnp.arange(ADAPTER_POOL, dtype=jnp.int32)
    order = jnp.argsort(owners_all * ADAPTER_POOL + adapter_ids, stable=True).astype(jnp.int32)
    device_keys = jax.random.split(jax.random.fold_in(key, 602), groups)

    def one_group(group_key):
        first_key, second_key, third_key, fourth_key, fifth_key = jax.random.split(group_key, 5)
        index = jnp.arange(NB, dtype=jnp.int32)
        ranking = jnp.where(index < CAPQ, 0, 1 + (index - CAPQ) % (groups - 1))
        block_owner = jax.random.permutation(first_key, groups)[ranking]
        block_owner = block_owner[jax.random.permutation(second_key, NB)]
        pick = jax.random.randint(third_key, (NB,), 0, APR)
        adapters = order[block_owner * APR + pick]
        offset = jax.random.randint(fourth_key, (NB // 2,), 1 - BAVG, BAVG)
        offset = offset.at[0].set(BAVG - 1)
        sizes_pair = jnp.stack([BAVG + offset, BAVG - offset], axis=1).reshape(NB)
        sizes_pair = sizes_pair[jax.random.permutation(fifth_key, NB)]
        starts = (jnp.cumsum(sizes_pair) - sizes_pair).astype(jnp.int32)
        local_rows = jnp.arange(ROWS, dtype=jnp.int32)
        row_block = jnp.sum((starts[None, :] <= local_rows[:, None]).astype(jnp.int32), axis=1) - 1
        return (adapters[row_block].astype(jnp.int32), starts)
    row_map, start_map = jax.vmap(one_group)(device_keys)
    return (owners_all, row_map.reshape(-1), start_map.reshape(-1))


def draw_adapter_owner_group(key, part):
    owners_all, row_map, start_map = block_layout(key)
    return owners_all


def draw_request_adapter(key, part):
    owners_all, row_map, start_map = block_layout(key)
    return row_map


def draw_block_first_row(key, part):
    owners_all, row_map, start_map = block_layout(key)
    return start_map


def draw_lengths(key, part):
    key = jax.random.fold_in(key, 7)
    drawn = jax.random.randint(key, (ROWS_ALL,), 2, CACHE + 1)
    return drawn.at[::ROWS].set(CACHE).astype(jnp.int32)


def draw_key_cache_rows(key, part):
    keys_drawn = shared_keys(key)
    return keys_drawn.astype(jnp.bfloat16)


def draw_queries(key, part):
    key = jax.random.fold_in(key, 5)
    drawn = jnp.clip(jax.random.normal(key, (ROWS_ALL, STEPS, QH * HD), jnp.float32), -6.0, 6.0)
    return drawn.astype(jnp.bfloat16)


def steps_of(stream_key, shape, pieces, least, top_value):
    factor_of = 1.0
    for dim, blocks in pieces:
        draws = jax.random.uniform(jax.random.fold_in(jax.random.fold_in(stream_key, 6), dim), (blocks,), jnp.float32, least / len(pieces), top_value / len(pieces))
        factor_of = factor_of * jnp.repeat(jnp.exp(draws), shape[dim] // blocks).reshape((-1,) + (1,) * (len(shape) - 1 - dim))
    return factor_of


def scatter_about(stream_key, dims, scale, bound, shards=(), held_as=jnp.bfloat16):
    values = scale * jax.random.normal(stream_key, dims, jnp.float32)
    if shards:
        values = values * steps_of(stream_key, dims, shards, -0.22, 0.18)
    return jnp.clip(values, -bound, bound).astype(held_as)


def setup_inputs(seed: int = 0) -> dict:
    seeds = jax.random.split(jax.random.key(seed), 12)
    hidden = scatter_about(seeds[0], (ROWS_ALL, STEPS, MODEL_WIDTH), 1.0, 6.0, ((0, 32), (2, 8)))
    queries = draw_queries(jax.random.fold_in(seeds[11], 71), 0)
    key_cache_rows = draw_key_cache_rows(jax.random.fold_in(seeds[11], 71), 0)
    value_cache_rows = scatter_about(seeds[3], (ROWS_ALL, CACHE, KEY_FEATURES), 1.0, 6.0, ((0, 32), (2, 8)))
    lengths = draw_lengths(jax.random.fold_in(seeds[11], 71), 0)
    request_adapter = draw_request_adapter(jax.random.fold_in(seeds[11], 71), 0)
    block_first_row = draw_block_first_row(jax.random.fold_in(seeds[11], 71), 0)
    adapter_owner_group = draw_adapter_owner_group(jax.random.fold_in(seeds[11], 71), 0)
    key_value_weight = scatter_about(seeds[8], (MODEL_WIDTH, 2, KEY_FEATURES), MODEL_WIDTH ** -0.5, 0.0625, ((2, 8),))
    adapter_down_weight = scatter_about(seeds[9], (ADAPTER_POOL, 2, ADAPTER_RANK, MODEL_WIDTH), MODEL_WIDTH ** -0.5, 0.0625, ((0, 32), (3, 8)))
    adapter_up_weight = scatter_about(seeds[10], (ADAPTER_POOL, 2, ADAPTER_RANK, KEY_FEATURES), ADAPTER_RANK ** -0.5, 1.0, ((0, 32), (3, 8)))
    return {"hidden": hidden, "queries": queries, "key_cache_rows": key_cache_rows, "value_cache_rows": value_cache_rows, "lengths": lengths, "request_adapter": request_adapter, "block_first_row": block_first_row, "adapter_owner_group": adapter_owner_group, "key_value_weight": key_value_weight, "adapter_down_weight": adapter_down_weight, "adapter_up_weight": adapter_up_weight}


masked_score = -1e30


def store_positions(adapter_owner_group):
    adapter_ids = jnp.arange(adapter_owner_group.shape[0], dtype=jnp.int32)
    earlier = (adapter_owner_group[None, :] == adapter_owner_group[:, None]) & (adapter_ids[None, :] < adapter_ids[:, None])
    return (adapter_owner_group * APR + jnp.sum(earlier.astype(jnp.int32), axis=1)).astype(jnp.int32)


def attend_block(query_block, key_block, value_block, length_block, fresh_block):
    row_count = query_block.shape[0]
    step_count = query_block.shape[1]
    query_heads = query_block.reshape(row_count, step_count, KVH, QH // KVH, HD).astype(jnp.float32)
    old_keys = key_block.reshape(row_count, CACHE, KVH, HD).astype(jnp.float32)
    old_values = value_block.reshape(row_count, CACHE, KVH, HD).astype(jnp.float32)
    new_keys = fresh_block[:, :, 0].reshape(row_count, step_count, KVH, HD).astype(jnp.float32)
    new_values = fresh_block[:, :, 1].reshape(row_count, step_count, KVH, HD).astype(jnp.float32)
    scale = HD ** -0.5
    cached_scores = jnp.einsum('rsgjh,rpgh->rsgjp', query_heads, old_keys) * scale
    fresh_scores = jnp.einsum('rsgjh,rtgh->rsgjt', query_heads, new_keys) * scale
    live = jnp.arange(CACHE)[None, :] < length_block[:, None]
    cached_scores = jnp.where(live[:, None, None, None, :], cached_scores, masked_score)
    causal = jnp.arange(step_count)[None, :] <= jnp.arange(step_count)[:, None]
    fresh_scores = jnp.where(causal[None, :, None, None, :], fresh_scores, masked_score)
    highest = jnp.maximum(jnp.max(cached_scores, axis=-1), jnp.max(fresh_scores, axis=-1))
    cached_exp = jnp.exp(cached_scores - highest[..., None])
    fresh_exp = jnp.exp(fresh_scores - highest[..., None])
    total = jnp.sum(cached_exp, axis=-1) + jnp.sum(fresh_exp, axis=-1)
    cached_probs = (cached_exp / total[..., None]).astype(jnp.bfloat16).astype(jnp.float32)
    fresh_probs = (fresh_exp / total[..., None]).astype(jnp.bfloat16).astype(jnp.float32)
    mixed = jnp.einsum('rsgjp,rpgh->rsgjh', cached_probs, old_values) + jnp.einsum('rsgjt,rtgh->rsgjh', fresh_probs, new_values)
    return mixed.astype(jnp.bfloat16).reshape(row_count, step_count, QH * HD)


def reference(hidden, queries, key_cache_rows, value_cache_rows, lengths, request_adapter, block_first_row, adapter_owner_group, key_value_weight, adapter_down_weight, adapter_up_weight):
    groups = ROWS_ALL // ROWS
    position = store_positions(adapter_owner_group)
    starts = block_first_row.reshape(groups, NB)
    local_rows = jnp.arange(ROWS, dtype=jnp.int32)
    row_block = jnp.sum((starts[:, None, :] <= local_rows[None, :, None]).astype(jnp.int32), axis=2) - 1
    first_row = jnp.take_along_axis(starts, row_block, axis=1)
    group_base = (jnp.arange(groups, dtype=jnp.int32) * ROWS)[:, None]
    used_adapter = request_adapter[(group_base + first_row).reshape(-1)]
    row_store = position[used_adapter]
    base = jnp.dot(hidden.reshape(-1, MODEL_WIDTH), key_value_weight.reshape(MODEL_WIDTH, -1), preferred_element_type=jnp.float32)
    base = base.reshape(ROWS_ALL, STEPS, 2, KEY_FEATURES)

    def one_row(inputs):
        features, store_slot = inputs
        down_mapping = adapter_down_weight[store_slot].astype(jnp.float32)
        up_mapping = adapter_up_weight[store_slot].astype(jnp.float32)
        low = jnp.einsum('sd,cid->sci', features.astype(jnp.float32), down_mapping).astype(jnp.bfloat16)
        return jnp.einsum('sci,cik->sck', low.astype(jnp.float32), up_mapping)

    delta = lax.map(one_row, (hidden, row_store))
    fresh_kv = (base + delta).astype(jnp.bfloat16)

    def one_group(inputs):
        return attend_block(*inputs)

    attended = lax.map(one_group, (queries.reshape(groups, ROWS, STEPS, QH * HD),
                                   key_cache_rows.reshape(groups, ROWS, CACHE, KEY_FEATURES),
                                   value_cache_rows.reshape(groups, ROWS, CACHE, KEY_FEATURES),
                                   lengths.reshape(groups, ROWS),
                                   fresh_kv.reshape(groups, ROWS, STEPS, 2, KEY_FEATURES)))
    return fresh_kv, attended.reshape(ROWS_ALL, STEPS, QH * HD)
```

```python
import jax
import jax.numpy as jnp
from jax import lax
from jax.sharding import PartitionSpec as P

HD = 128
BLK = 7
PAIR = 2
PAIR_ROWS = PAIR * BLK


masked_score = -1e30


def attend_local(queries, key_cache_rows, value_cache_rows, lengths, fresh):
    row_count = queries.shape[0]
    step_count = queries.shape[1]
    head_count = fresh.shape[3] // HD
    query_heads = queries.reshape(row_count, step_count, head_count, -1, HD)
    old_keys = key_cache_rows.reshape(row_count, -1, head_count, HD)
    old_values = value_cache_rows.reshape(row_count, -1, head_count, HD)
    new_keys = fresh[:, :, 0].reshape(row_count, step_count, head_count, HD)
    new_values = fresh[:, :, 1].reshape(row_count, step_count, head_count, HD)
    scale = HD ** (-0.5)
    cached_scores = (
        jnp.einsum("rsgjh,rpgh->rsgjp", query_heads, old_keys, preferred_element_type=jnp.float32)
        * scale
    )
    fresh_scores = (
        jnp.einsum("rsgjh,rtgh->rsgjt", query_heads, new_keys, preferred_element_type=jnp.float32)
        * scale
    )
    live = jnp.arange(old_keys.shape[1])[None, :] < lengths[:, None]
    cached_scores = jnp.where(live[:, None, None, None, :], cached_scores, masked_score)
    causal = jnp.arange(step_count)[None, :] <= jnp.arange(step_count)[:, None]
    fresh_scores = jnp.where(causal[None, :, None, None, :], fresh_scores, masked_score)
    highest = jnp.maximum(jnp.max(cached_scores, axis=-1), jnp.max(fresh_scores, axis=-1))
    cached_exp = jnp.exp(cached_scores - highest[..., None])
    fresh_exp = jnp.exp(fresh_scores - highest[..., None])
    total = jnp.sum(cached_exp, axis=-1) + jnp.sum(fresh_exp, axis=-1)
    cached_probs = (cached_exp / total[..., None]).astype(jnp.bfloat16)
    fresh_probs = (fresh_exp / total[..., None]).astype(jnp.bfloat16)
    mixed = jnp.einsum(
        "rsgjp,rpgh->rsgjh", cached_probs, old_values, preferred_element_type=jnp.float32
    )
    mixed = mixed + jnp.einsum(
        "rsgjt,rtgh->rsgjh", fresh_probs, new_values, preferred_element_type=jnp.float32
    )
    return mixed.astype(jnp.bfloat16).reshape(row_count, step_count, -1)


def shifted(value, dx, dy):
    pairs = [(t, ((t // 2 + dx) % 4) * 2 + ((t % 2) ^ dy)) for t in range(8)]
    return lax.ppermute(value, "tensor", pairs)


def sum_over_tensor(value):
    value = value + shifted(value, 0, 1)
    return (value + shifted(value, 2, 0)) + (shifted(value, 1, 0) + shifted(value, -1, 0))


def project(tokens, key_value_weight):
    half = tokens.shape[0] // 2
    here = lax.axis_index("tensor")
    x, y = here // 2, here % 2
    depth = tokens.shape[1]

    def product(piece, dx, dy):
        start = (lax.rem(x - dx + 4, 4) * 2 + (y ^ dy)) * depth
        part = lax.dynamic_slice_in_dim(key_value_weight, start, depth, 0)
        return jnp.einsum("td,dck->tck", piece, part, preferred_element_type=jnp.float32)

    right = shifted(tokens, 1, 0)
    left = shifted(tokens, -1, 0)
    across = shifted(tokens, 0, 1)
    right_across = shifted(across, 1, 0)
    left_across = shifted(across, -1, 0)
    far = jnp.concatenate([shifted(right[:half], 1, 0), shifted(left[half:], -1, 0)], axis=0)
    far_across = shifted(far, 0, 1)
    base = product(tokens, 0, 0) + product(across, 0, 1)
    base = base + product(right, 1, 0) + product(left, -1, 0)
    base = base + product(right_across, 1, 1) + product(left_across, -1, 1)
    return base + product(far, 2, 0) + product(far_across, 2, 1)


def per_device(
    hidden,
    queries,
    key_cache_rows,
    value_cache_rows,
    lengths,
    request_adapter,
    block_first_row,
    adapter_owner_group,
    key_value_weight,
    adapter_down_weight,
    adapter_up_weight,
):
    row_count, step_count, depth = hidden.shape
    replicas = lax.axis_size("replica")
    block_count = block_first_row.shape[0]
    token_count = row_count * step_count
    held, sides, rank = adapter_down_weight.shape[:3]
    tokens = hidden.reshape(token_count, depth)

    rows = jnp.arange(row_count, dtype=jnp.int32)
    pool = jnp.arange(adapter_owner_group.shape[0], dtype=jnp.int32)
    first = block_first_row
    after = jnp.concatenate([first[1:], jnp.full((1,), row_count, jnp.int32)])
    block_adapter = jnp.sum(
        jnp.where(first[:, None] == rows[None, :], request_adapter[None, :], 0), axis=1
    )
    block_owner = jnp.sum(
        jnp.where(block_adapter[:, None] == pool[None, :], adapter_owner_group[None, :], 0), axis=1
    )
    block_slot = jnp.sum(
        (adapter_owner_group[None, :] == block_owner[:, None]) & (pool[None, :] < block_adapter[:, None]),
        axis=1, dtype=jnp.int32,
    )
    ids = jnp.arange(block_count, dtype=jnp.int32)
    before = (block_owner[None, :] == block_owner[:, None]) & (ids[None, :] < ids[:, None])
    block_turn = jnp.sum(before, axis=1, dtype=jnp.int32)
    block_offset = jnp.sum(jnp.where(before, (after - first)[None, :], 0), axis=1)

    member = (first[None, :] <= rows[:, None]) & (rows[:, None] < after[None, :])
    row_place = rows + jnp.sum(
        jnp.where(member, (block_owner * PAIR_ROWS + block_offset - first)[None, :], 0), axis=1
    )
    row_slot = jnp.sum(jnp.where(member, block_slot[None, :], 0), axis=1)
    row_fetch = jnp.sum(jnp.where(member, (block_owner * PAIR + block_turn)[None, :], 0), axis=1)
    places = jnp.arange(replicas * PAIR_ROWS, dtype=jnp.int32)
    place_slot = jnp.sum(jnp.where(places[:, None] == row_place[None, :], row_slot[None, :], 0), axis=1)
    fetches = jnp.arange(replicas * PAIR, dtype=jnp.int32)
    fetch_slot = jnp.sum(
        jnp.where(fetches[:, None] == (block_owner * PAIR + block_turn)[None, :], block_slot[None, :], 0),
        axis=1,
    )
    wanted = lax.all_gather(jnp.concatenate([place_slot, fetch_slot]), "replica", axis=0)

    token_place = (row_place[:, None] * step_count + jnp.arange(step_count, dtype=jnp.int32)[None, :]).reshape(-1)
    token_places = jnp.arange(replicas * PAIR_ROWS * step_count, dtype=jnp.int32)
    sent = jnp.dot(
        (token_places[:, None] == token_place[None, :]).astype(jnp.bfloat16), tokens,
        preferred_element_type=jnp.float32,
    ).astype(jnp.bfloat16)
    received = lax.all_to_all(
        sent.reshape(replicas, PAIR_ROWS * step_count, depth), "replica", split_axis=0, concat_axis=0, tiled=True
    ).reshape(-1, depth)

    me = lax.axis_index("replica")
    received_slot = lax.dynamic_slice(wanted, (0, me * PAIR_ROWS), (replicas, PAIR_ROWS))
    asked_slot = lax.dynamic_slice(
        wanted, (0, replicas * PAIR_ROWS + me * PAIR), (replicas, PAIR)
    )
    up_fetched = lax.all_to_all(
        adapter_up_weight[asked_slot], "replica", split_axis=0, concat_axis=0, tiled=True
    ).reshape(replicas * PAIR, sides, rank, -1)

    base = project(tokens, key_value_weight)

    every = jnp.einsum(
        "td,acid->taci", received, adapter_down_weight, preferred_element_type=jnp.float32
    )
    token_slot = jnp.repeat(received_slot.reshape(-1), step_count)
    chosen = token_slot[:, None] == jnp.arange(held, dtype=jnp.int32)[None, :]
    partial_low = jnp.sum(jnp.where(chosen[:, :, None, None], every, 0.0), axis=1)
    returned = lax.all_to_all(
        partial_low.reshape(replicas, -1, 128), "replica", split_axis=0, concat_axis=0, tiled=True
    ).reshape(-1, sides * rank)
    mine = returned[token_place]
    low = sum_over_tensor(mine.reshape(-1, 128)).astype(jnp.bfloat16).reshape(token_count, sides, rank)

    token_fetch = jnp.repeat(row_fetch, step_count)
    spread = jnp.where(
        (token_fetch[:, None] == fetches[None, :])[:, None, :, None], low[:, :, None, :], 0
    ).astype(jnp.bfloat16)
    delta = jnp.einsum("tcui,ucif->tcf", spread, up_fetched, preferred_element_type=jnp.float32)
    fresh = (base + delta).astype(jnp.bfloat16).reshape(row_count, step_count, sides, -1)
    attended = attend_local(queries, key_cache_rows, value_cache_rows, lengths, fresh)
    return (fresh, attended)


def solution(mesh):
    placed = (
        P("replica", None, "tensor"),
        P("replica", None, "tensor"),
        P("replica", None, "tensor"),
        P("replica", None, "tensor"),
        P("replica"),
        P("replica"),
        P("replica"),
        P(),
        P(None, None, "tensor"),
        P("replica", None, None, "tensor"),
        P("replica", None, None, "tensor"),
    )
    return jax.shard_map(
        per_device,
        mesh=mesh,
        in_specs=placed,
        out_specs=(P("replica", None, None, "tensor"), P("replica", None, "tensor")),
        check_vma=False,
    )
```

```python
import functools

import jax
import jax.numpy as jnp
from jax import lax
from jax.experimental import pallas as pl
from jax.experimental.pallas import tpu as pltpu
from jax.sharding import PartitionSpec as P

HD = 128
BLK = 7
PAIR = 2
PAIR_ROWS = PAIR * BLK
SPAN = PAIR_ROWS + PAIR
GROUP = 8

masked_score = -1e30


def iota(shape, dim):
    return lax.broadcasted_iota(jnp.int32, shape, dim)


def total(value, axis):
    return jnp.sum(value, axis=axis, keepdims=True)


def place_kernel(steps, first_ref, request_ref, owner_ref, tokens_ref, sent_ref, wanted_ref, column_ref, fetch_ref, row_ref):
    part = sent_ref.shape[0]
    token_count = tokens_ref.shape[0]

    @pl.when(pl.program_id(0) == 0)
    def _():
        first = first_ref[...]
        blocks = first.shape[1]
        rows = request_ref.shape[1]
        pool = owner_ref.shape[1]
        owners = owner_ref[...]
        i, j = iota((blocks, blocks), 0), iota((blocks, blocks), 1)

        def down(value):
            return total(jnp.where(i == j, value, 0), 1)

        def across(value):
            return total(jnp.where(i == j, value, 0), 0)

        first_c = down(first)
        after_c = total(jnp.where(j == i + 1, first, 0), 1) + jnp.where(i[:, :1] == blocks - 1, rows, 0)
        after = across(after_c)
        adapter_c = total(jnp.where(iota((blocks, rows), 1) == first_c, request_ref[...], 0), 1)
        ids = iota((blocks, pool), 1)
        owner_c = total(jnp.where(ids == adapter_c, owners, 0), 1)
        slot_c = total(jnp.where((owners == owner_c) & (ids < adapter_c), 1, 0), 1)
        owner, slot = across(owner_c), across(slot_c)
        before = (owner == owner_c) & (j < i)
        turn_c = total(jnp.where(before, 1, 0), 1)
        offset_c = total(jnp.where(before, after - first, 0), 1)
        turn, offset = across(turn_c), across(offset_c)

        r, b = iota((rows, blocks), 0), iota((rows, blocks), 1)
        member = (first <= r) & (r < after)
        spot = r[:, :1] + total(jnp.where(member, owner * SPAN + offset - first, 0), 1)
        row_slot = total(jnp.where(member, slot, 0), 1)
        lanes = wanted_ref.shape[1]
        wanted = total(jnp.where(iota((rows, lanes), 1) == spot, row_slot, 0), 0)
        asked = owner_c * SPAN + PAIR_ROWS + turn_c
        wanted_ref[...] = wanted + total(jnp.where(iota((blocks, lanes), 1) == asked, slot_c, 0), 0)

        t = iota((blocks, token_count), 1)
        member = (first_c * steps <= t) & (t < after_c * steps)
        row_ref[...] = t[:1] + total(
            jnp.where(member, (owner_c * PAIR_ROWS + offset_c - first_c) * steps, 0), 0
        )
        t = iota((token_count, blocks), 0)
        member = (first * steps <= t) & (t < after * steps)
        column_ref[...] = t[:, :1] + total(
            jnp.where(member, (owner * PAIR_ROWS + offset - first) * steps, 0), 1
        )
        fetch_ref[...] = total(jnp.where(member, owner * PAIR + turn, 0), 1)

    spots = iota((part, token_count), 0) + pl.program_id(0) * part
    pick = jnp.where(spots == row_ref[...], 1.0, 0.0).astype(jnp.bfloat16)
    sent_ref[...] = jnp.dot(pick, tokens_ref[...], preferred_element_type=jnp.float32).astype(jnp.bfloat16)


def place(first, request, owners, tokens, steps, replicas):
    token_count, depth = tokens.shape
    sent_count = replicas * PAIR_ROWS * steps
    part = sent_count // 7
    whole = lambda shape: pl.BlockSpec(shape, lambda i: (0, 0))
    return pl.pallas_call(
        functools.partial(place_kernel, steps),
        grid=(7,),
        in_specs=[
            whole((1, first.shape[0])), whole((1, request.shape[0])), whole((1, owners.shape[0])),
            whole((token_count, depth)),
        ],
        out_specs=[
            pl.BlockSpec((part, depth), lambda i: (i, 0)), whole((1, replicas * SPAN)),
            whole((token_count, 1)), whole((token_count, 1)),
        ],
        out_shape=[
            jax.ShapeDtypeStruct((sent_count, depth), jnp.bfloat16),
            jax.ShapeDtypeStruct((1, replicas * SPAN), jnp.int32),
            jax.ShapeDtypeStruct((token_count, 1), jnp.int32),
            jax.ShapeDtypeStruct((token_count, 1), jnp.int32),
        ],
        scratch_shapes=[pltpu.VMEM((1, token_count), jnp.int32)],
        compiler_params=pltpu.CompilerParams(vmem_limit_bytes=24 * 2**20),
        name="place_rows",
    )(first[None], request[None], owners[None], tokens)


def rank_kernel(steps, slots_ref, rows_ref, maps_ref, out_ref):
    part = rows_ref.shape[0]
    width = out_ref.shape[1] // 2
    every = lax.dot_general(
        rows_ref[...], maps_ref[...], (((1,), (1,)), ((), ())), preferred_element_type=jnp.float32
    )
    i = iota((part, 1), 0)
    each = PAIR_ROWS * steps
    source = i // each
    lane = (source + pl.program_id(0) * (part // each)) * SPAN + (i - source * each) // steps
    lanes = slots_ref.shape[1]
    slot = total(jnp.where(iota((part, lanes), 1) == lane, slots_ref[...], 0), 1)
    two = jnp.zeros((part, 2 * width), jnp.float32)
    for pair in range(every.shape[1] // (2 * width)):
        two = jnp.where(slot // 2 == pair, every[:, pair * 2 * width:(pair + 1) * 2 * width], two)
    own = jnp.where(slot % 2 == 1, two[:, width:], two[:, :width])
    high = own.astype(jnp.bfloat16)
    low = (own - high.astype(jnp.float32)).astype(jnp.bfloat16)
    out_ref[...] = jnp.concatenate([high, low], axis=1)


def rank_products(slots, rows, maps, steps, width):
    count, depth = rows.shape
    part = count // 8
    return pl.pallas_call(
        functools.partial(rank_kernel, steps),
        grid=(8,),
        in_specs=[
            pl.BlockSpec(slots.shape, lambda i: (0, 0)), pl.BlockSpec((part, depth), lambda i: (i, 0)),
            pl.BlockSpec(maps.shape, lambda i: (0, 0)),
        ],
        out_specs=pl.BlockSpec((part, 2 * width), lambda i: (i, 0)),
        out_shape=jax.ShapeDtypeStruct((count, 2 * width), jnp.bfloat16),
        compiler_params=pltpu.CompilerParams(vmem_limit_bytes=24 * 2**20),
        cost_estimate=pl.CostEstimate(flops=2 * count * depth * maps.shape[0], bytes_accessed=6 * 2**20, transcendentals=0),
        name="rank_products",
    )(slots, rows, maps)


def collect_kernel(column_ref, returned_ref, out_ref):
    tokens, width = column_ref.shape[0], returned_ref.shape[1] // 2
    pick = jnp.where(iota((tokens, returned_ref.shape[0]), 1) == column_ref[...], 1.0, 0.0).astype(jnp.bfloat16)
    both = jnp.dot(pick, returned_ref[...], preferred_element_type=jnp.float32)
    value = both[:, :width] + both[:, width:]
    out_ref[...] = jnp.concatenate([value[: tokens // 2], value[tokens // 2:]], axis=1)


def collect(column, returned):
    tokens, width = column.shape[0], returned.shape[1]
    return pl.pallas_call(
        collect_kernel,
        out_shape=jax.ShapeDtypeStruct((tokens // 2, width), jnp.float32),
        compiler_params=pltpu.CompilerParams(vmem_limit_bytes=24 * 2**20),
        name="collect",
    )(column, returned)


def heads_first(value, heads):
    return jnp.concatenate([value[:, h * HD:(h + 1) * HD] for h in range(heads)], axis=0)


def cached_kernel(steps, bias_ref, queries_ref, keys_ref, values_ref, mixed_ref, weight_ref):
    heads = queries_ref.shape[1] // HD
    rows = keys_ref.shape[0] // GROUP if keys_ref.ndim == 3 else 1
    cache = keys_ref.shape[1]
    count = GROUP * steps
    for g in range(rows):
        query = heads_first(queries_ref[g * count:(g + 1) * count, :], heads)
        keys = keys_ref[g * GROUP:(g + 1) * GROUP].reshape(GROUP * cache, HD)
        values = values_ref[g * GROUP:(g + 1) * GROUP].reshape(GROUP * cache, HD)
        score = lax.dot_general(query, keys, (((1,), (1,)), ((), ())), preferred_element_type=jnp.float32)
        shape = score.shape
        own = (iota(shape, 0) // steps) % GROUP == iota(shape, 1) // cache
        score = jnp.where(own, score * HD ** -0.5 + bias_ref[g], masked_score)
        highest = jnp.max(score, axis=1, keepdims=True)
        exped = jnp.exp(score - highest)
        summed = total(exped, 1)
        mixed = jnp.dot(exped.astype(jnp.bfloat16), values, preferred_element_type=jnp.float32)
        mixed_ref[g] = mixed / summed
        weight_ref[g] = jnp.broadcast_to(highest + jnp.log(summed), mixed.shape)


def cached_attention(lengths, queries, keys, values, steps):
    rows, cache = keys.shape[:2]
    heads = queries.shape[1] // HD
    groups = rows // GROUP
    count = GROUP * steps * heads
    live = jnp.arange(cache, dtype=jnp.int32)[None, :] < lengths[:, None]
    bias = jnp.where(live, 0.0, masked_score).astype(jnp.float32).reshape(groups, 1, GROUP * cache)
    per = 2
    return pl.pallas_call(
        functools.partial(cached_kernel, steps),
        grid=(groups // per,),
        in_specs=[
            pl.BlockSpec((per, 1, GROUP * cache), lambda i: (i, 0, 0)),
            pl.BlockSpec((per * GROUP * steps, heads * HD), lambda i: (i, 0)),
            pl.BlockSpec((per * GROUP, cache, HD), lambda i: (i, 0, 0)),
            pl.BlockSpec((per * GROUP, cache, HD), lambda i: (i, 0, 0)),
        ],
        out_specs=[pl.BlockSpec((per, count, HD), lambda i: (i, 0, 0))] * 2,
        out_shape=[jax.ShapeDtypeStruct((groups, count, HD), jnp.float32)] * 2,
        compiler_params=pltpu.CompilerParams(vmem_limit_bytes=24 * 2**20),
        cost_estimate=pl.CostEstimate(flops=2**31, bytes_accessed=8 * 2**20, transcendentals=2**20),
        name="cached_attention",
    )(bias, queries, keys, values)


def finish_kernel(steps, rank, fetch_ref, a_ref, b_ref, c_ref, d_ref, maps_ref, base_ref, queries_ref, mixed_ref, weight_ref, fresh_ref, out_ref, held_ref):
    heads = queries_ref.shape[1] // HD
    count = GROUP * steps
    tokens = fetch_ref.shape[0]

    @pl.when(pl.program_id(0) == 0)
    def _():
        summed = (a_ref[...] + b_ref[...]) + (c_ref[...] + d_ref[...])
        width = summed.shape[1] // 2
        low = jnp.concatenate([summed[:, :width], summed[:, width:]], axis=0)
        fetch = fetch_ref[...]
        lanes = iota((tokens, 128), 1) // rank
        for side in range(2):
            four = jnp.concatenate([low[:, side * rank:(side + 1) * rank]] * (128 // rank), axis=1)
            spread = jnp.concatenate(
                [
                    jnp.where(fetch == lanes + k * (128 // rank), four, 0.0).astype(jnp.bfloat16)
                    for k in range(maps_ref.shape[1] // 128)
                ],
                axis=1,
            )
            delta = jnp.dot(spread, maps_ref[side], preferred_element_type=jnp.float32)
            new = base_ref[:, side * HD:(side + 1) * HD] + delta
            held_ref[:, side * HD:(side + 1) * HD] = new.astype(jnp.bfloat16)
        fresh_ref[...] = held_ref[...]

    for g in range(mixed_ref.shape[0]):
        start = pl.multiple_of((pl.program_id(0) * mixed_ref.shape[0] + g) * count, count)
        new = held_ref[pl.ds(start, count), :]
        query = heads_first(queries_ref[g * count:(g + 1) * count, :], heads)
        score = lax.dot_general(
            query, new[:, :HD], (((1,), (1,)), ((), ())), preferred_element_type=jnp.float32
        )
        i, j = iota(score.shape, 0), iota(score.shape, 1)
        seen = ((i // steps) % GROUP == j // steps) & (j % steps <= i % steps)
        score = jnp.where(seen, score * HD ** -0.5, masked_score)
        weight = weight_ref[g][:, :1]
        highest = jnp.maximum(jnp.max(score, axis=1, keepdims=True), weight)
        exped = jnp.exp(score - highest)
        cached = jnp.exp(weight - highest)
        summed = total(exped, 1) + cached
        probs = (exped / summed).astype(jnp.bfloat16)
        mixed = mixed_ref[g] * (cached / summed) + jnp.dot(
            probs, new[:, HD:], preferred_element_type=jnp.float32
        )
        mixed = mixed.astype(jnp.bfloat16)
        for h in range(heads):
            out_ref[g * count:(g + 1) * count, h * HD:(h + 1) * HD] = mixed[h * count:(h + 1) * count]


def finish(fetch, parts, maps, base, queries, mixed, weight, steps, rank):
    tokens, features = queries.shape
    groups, rows = mixed.shape[:2]
    per = 2
    whole = lambda x: pl.BlockSpec(x.shape, lambda i: (0,) * x.ndim)
    block = pl.BlockSpec((per * GROUP * steps, features), lambda i: (i, 0))
    return pl.pallas_call(
        functools.partial(finish_kernel, steps, rank),
        grid=(groups // per,),
        in_specs=[whole(fetch)] + [whole(p) for p in parts] + [whole(maps), whole(base), block]
        + [pl.BlockSpec((per, rows, HD), lambda i: (i, 0, 0))] * 2,
        out_specs=[pl.BlockSpec(base.shape, lambda i: (0, 0)), block],
        out_shape=[
            jax.ShapeDtypeStruct(base.shape, jnp.bfloat16),
            jax.ShapeDtypeStruct((tokens, features), jnp.bfloat16),
        ],
        scratch_shapes=[pltpu.VMEM(base.shape, jnp.bfloat16)],
        compiler_params=pltpu.CompilerParams(vmem_limit_bytes=32 * 2**20),
        name="finish",
    )(fetch, *parts, maps, base, queries, mixed, weight)


def shifted(value, dx, dy):
    pairs = [(t, ((t // 2 + dx) % 4) * 2 + ((t % 2) ^ dy)) for t in range(8)]
    return lax.ppermute(value, "tensor", pairs)


def exchange(value):
    me = lax.axis_index("replica")
    y, z, core = me >> 4, (me >> 1) & 7, me & 1
    rest = value.shape[1:]
    value = value.reshape((2, 8, 2) + rest)

    def send(piece, move):
        pairs = []
        for k in range(32):
            to_y, to_z, to_core = move(k >> 4, (k >> 1) & 7, k & 1)
            pairs.append((k, to_y * 16 + (to_z % 8) * 2 + to_core))
        return lax.ppermute(piece, "replica", pairs)

    pieces = [lax.dynamic_index_in_dim(value, (z + k) & 7, 1, keepdims=False) for k in range(8)]
    arrived = [pieces[0]] + [
        send(pieces[k], lambda a, b, c, k=k: (a, b + k, c)) for k in range(1, 8)
    ]
    turned = jnp.stack([arrived[(-k) % 8] for k in range(8)], axis=0)
    value = lax.dynamic_slice_in_dim(jnp.concatenate([turned, turned], axis=0), 8 - z, 8, 0)
    other = send(lax.dynamic_index_in_dim(value, 1 - y, 1, keepdims=False), lambda a, b, c: (1 - a, b, c))
    own = lax.dynamic_index_in_dim(value, y, 1, keepdims=False)
    value = jnp.where(y == 0, jnp.stack([own, other]), jnp.stack([other, own]))
    other = send(lax.dynamic_index_in_dim(value, 1 - core, 2, keepdims=False), lambda a, b, c: (a, b, 1 - c))
    own = lax.dynamic_index_in_dim(value, core, 2, keepdims=False)
    value = jnp.where(core == 0, jnp.stack([own, other], axis=2), jnp.stack([other, own], axis=2))
    return value.reshape((32,) + rest)


def project(tokens, key_value_weight):
    half = tokens.shape[0] // 2
    here = lax.axis_index("tensor")
    x, y = here >> 1, here & 1
    depth = tokens.shape[1]

    def product(piece, dx, dy):
        start = ((((x - dx) & 3) << 1) | (y ^ dy)) * depth
        part = lax.dynamic_slice_in_dim(key_value_weight, start, depth, 0)
        return jnp.dot(piece, part.reshape(depth, -1), preferred_element_type=jnp.float32)

    right = shifted(tokens, 1, 0)
    left = shifted(tokens, -1, 0)
    across = shifted(tokens, 0, 1)
    right_across = shifted(across, 1, 0)
    left_across = shifted(across, -1, 0)
    far = jnp.concatenate([shifted(right[:half], 1, 0), shifted(left[half:], -1, 0)], axis=0)
    far_across = shifted(far, 0, 1)
    base = product(tokens, 0, 0) + product(across, 0, 1)
    base = base + product(right, 1, 0) + product(left, -1, 0)
    base = base + product(right_across, 1, 1) + product(left_across, -1, 1)
    return base + product(far, 2, 0) + product(far_across, 2, 1)


def per_device(
    hidden,
    queries,
    key_cache_rows,
    value_cache_rows,
    lengths,
    request_adapter,
    block_first_row,
    adapter_owner_group,
    key_value_weight,
    adapter_down_weight,
    adapter_up_weight,
):
    row_count, steps, depth = hidden.shape
    replicas = lax.axis_size("replica")
    token_count = row_count * steps
    held, sides, rank = adapter_down_weight.shape[:3]
    tokens = hidden.reshape(token_count, depth)

    sent, wanted, column, fetch = place(
        block_first_row, request_adapter, adapter_owner_group, tokens, steps, replicas
    )
    received = lax.all_to_all(
        sent.reshape(replicas, PAIR_ROWS * steps, depth), "replica", split_axis=0, concat_axis=0, tiled=True
    ).reshape(-1, depth)
    wanted = exchange(wanted.reshape(replicas, SPAN))
    up_asked = adapter_up_weight[wanted[:, PAIR_ROWS:]].reshape(replicas, -1, HD)
    up = exchange(up_asked).reshape(replicas * PAIR, sides, rank, HD)
    up = up.transpose(1, 0, 2, 3).reshape(sides, replicas * PAIR * rank, HD)

    base = project(tokens, key_value_weight)
    query_tokens = queries.reshape(token_count, -1)
    mixed, weight = cached_attention(lengths, query_tokens, key_cache_rows, value_cache_rows, steps)

    products = rank_products(
        wanted.reshape(1, -1), received, adapter_down_weight.reshape(held * sides * rank, depth), steps, sides * rank
    )
    returned = lax.all_to_all(
        products.reshape(replicas, PAIR_ROWS * steps, -1), "replica", split_axis=0, concat_axis=0, tiled=True
    ).reshape(products.shape)
    mine = collect(column, returned)
    mine = mine + shifted(mine, 0, 1)
    parts = (mine, shifted(mine, 2, 0), shifted(mine, 1, 0), shifted(mine, -1, 0))
    fresh, attended = finish(fetch, parts, up, base, query_tokens, mixed, weight, steps, rank)
    return (
        fresh.reshape(row_count, steps, sides, HD),
        attended.reshape(row_count, steps, -1),
    )


def solution(mesh):
    placed = (
        P("replica", None, "tensor"),
        P("replica", None, "tensor"),
        P("replica", None, "tensor"),
        P("replica", None, "tensor"),
        P("replica"),
        P("replica"),
        P("replica"),
        P(),
        P(None, None, "tensor"),
        P("replica", None, None, "tensor"),
        P("replica", None, None, "tensor"),
    )
    return jax.shard_map(
        per_device,
        mesh=mesh,
        in_specs=placed,
        out_specs=(P("replica", None, None, "tensor"), P("replica", None, "tensor")),
        check_vma=False,
    )
```

```python
import functools

import jax
import jax.numpy as jnp
from jax import lax
from jax.experimental import pallas as pl
from jax.experimental.pallas import tpu as pltpu
from jax.sharding import PartitionSpec as P

HD = 128
BLK = 7
PAIR = 2
PAIR_ROWS = PAIR * BLK
ASK_ROWS = 16
RETURN_ROWS = 64
LANES = 128
GROUP = 8

masked_score = -1e30


def iota(shape, dim):
    return lax.broadcasted_iota(jnp.int32, shape, dim)


def total(value, axis):
    return jnp.sum(value, axis=axis, keepdims=True)


def place_kernel(steps, first_ref, request_ref, owner_ref, tokens_ref, sent_ref, column_ref, fetch_ref, row_ref, info_ref):
    here, _, lanes = sent_ref.shape
    each = PAIR_ROWS * steps
    token_count, depth = tokens_ref.shape

    @pl.when(pl.program_id(0) == 0)
    def _():
        first = first_ref[...]
        blocks = first.shape[1]
        rows = request_ref.shape[1]
        pool = owner_ref.shape[1]
        owners = owner_ref[...]
        i, j = iota((blocks, blocks), 0), iota((blocks, blocks), 1)

        def down(value):
            return total(jnp.where(i == j, value, 0), 1)

        def across(value):
            return total(jnp.where(i == j, value, 0), 0)

        first_c = down(first)
        after_c = total(jnp.where(j == i + 1, first, 0), 1) + jnp.where(i[:, :1] == blocks - 1, rows, 0)
        after = across(after_c)
        adapter_c = total(jnp.where(iota((blocks, rows), 1) == first_c, request_ref[...], 0), 1)
        ids = iota((blocks, pool), 1)
        owner_c = total(jnp.where(ids == adapter_c, owners, 0), 1)
        slot_c = total(jnp.where((owners == owner_c) & (ids < adapter_c), 1, 0), 1)
        owner, slot = across(owner_c), across(slot_c)
        before = (owner == owner_c) & (j < i)
        turn_c = total(jnp.where(before, 1, 0), 1)
        offset_c = total(jnp.where(before, after - first, 0), 1)
        turn, offset = across(turn_c), across(offset_c)

        r, b = iota((rows, blocks), 0), iota((rows, blocks), 1)
        member = (first <= r) & (r < after)
        spot = r[:, :1] + total(jnp.where(member, offset - first, 0), 1)
        row_slot = total(jnp.where(member, slot, 0), 1)
        r_row = iota((blocks, rows), 1)
        row_owner = total(jnp.where((first_c <= r_row) & (r_row < after_c), owner_c, 0), 0)
        count = info_ref.shape[0]
        goes = jnp.where(iota((count, rows), 0) == row_owner, 1.0, 0.0).astype(jnp.bfloat16)
        asks = jnp.where(iota((rows, lanes), 1) == spot, row_slot, 0).astype(jnp.float32).astype(jnp.bfloat16)
        info = jnp.dot(goes, asks, preferred_element_type=jnp.float32)
        goes = jnp.where(iota((count, blocks), 0) == owner, 1.0, 0.0).astype(jnp.bfloat16)
        asks = jnp.where(iota((blocks, lanes), 1) == PAIR_ROWS + turn_c, slot_c, 0)
        asks = asks.astype(jnp.float32).astype(jnp.bfloat16)
        info_ref[...] = info + jnp.dot(goes, asks, preferred_element_type=jnp.float32)

        t = iota((blocks, token_count), 1)
        member = (first_c * steps <= t) & (t < after_c * steps)
        row_ref[...] = t[:1] + total(
            jnp.where(member, (owner_c * PAIR_ROWS + offset_c - first_c) * steps, 0), 0
        )
        t = iota((token_count, blocks), 0)
        member = (first * steps <= t) & (t < after * steps)
        column_ref[...] = t[:, :1] + total(
            jnp.where(member, owner * RETURN_ROWS + (offset - first) * steps, 0), 1
        )
        fetch_ref[...] = total(jnp.where(member, owner * PAIR + turn, 0), 1)

    spots = iota((here * each, token_count), 0) + pl.program_id(0) * (here * each)
    pick = jnp.where(spots == row_ref[...], 1.0, 0.0).astype(jnp.bfloat16)
    picked = jnp.dot(pick, tokens_ref[...], preferred_element_type=jnp.float32)
    for k in range(here):
        asked = info_ref[pl.ds(pl.program_id(0) * here + k, 1), :]
        parts = [picked[k * each:(k + 1) * each, c * lanes:(c + 1) * lanes] for c in range(depth // lanes)]
        parts.append(jnp.where(iota((ASK_ROWS, lanes), 0) == 0, asked, 0.0))
        sent_ref[k] = jnp.concatenate(parts, axis=0).astype(jnp.bfloat16)


def place(first, request, owners, tokens, steps, replicas):
    token_count, depth = tokens.shape
    rows = PAIR_ROWS * steps * depth // LANES + ASK_ROWS
    here = 4
    whole = lambda shape: pl.BlockSpec(shape, lambda i: (0, 0))
    return pl.pallas_call(
        functools.partial(place_kernel, steps),
        grid=(replicas // here,),
        in_specs=[
            whole((1, first.shape[0])), whole((1, request.shape[0])), whole((1, owners.shape[0])),
            whole((token_count, depth)),
        ],
        out_specs=[
            pl.BlockSpec((here, rows, LANES), lambda i: (i, 0, 0)),
            whole((token_count, 1)), whole((token_count, 1)),
        ],
        out_shape=[
            jax.ShapeDtypeStruct((replicas, rows, LANES), jnp.bfloat16),
            jax.ShapeDtypeStruct((token_count, 1), jnp.int32),
            jax.ShapeDtypeStruct((token_count, 1), jnp.int32),
        ],
        scratch_shapes=[pltpu.VMEM((1, token_count), jnp.int32), pltpu.VMEM((replicas, LANES), jnp.float32)],
        compiler_params=pltpu.CompilerParams(vmem_limit_bytes=24 * 2**20),
        name="place_rows",
    )(first[None], request[None], owners[None], tokens)


def rank_kernel(steps, rows_ref, maps_ref, ups_ref, out_ref):
    here, _, lanes = rows_ref.shape
    each = PAIR_ROWS * steps
    width = lanes // 2
    depth = maps_ref.shape[0]
    tokens, slots, picks = [], [], []
    for k in range(here):
        got = rows_ref[k].astype(jnp.float32)
        chunks = [got[c * each:(c + 1) * each] for c in range(depth // lanes)]
        tokens.append(jnp.concatenate(chunks, axis=1))
        asked = got[each * (depth // lanes):][:1]
        shape = (each, lanes)
        slots.append(total(jnp.where(iota(shape, 1) == iota(shape, 0) // steps, asked, 0.0), 1))
        shape = (PAIR * width, ups_ref.shape[0])
        i = iota((PAIR * width, 1), 0)
        turn = total(jnp.where(iota((PAIR * width, lanes), 1) == PAIR_ROWS + i // width, asked, 0.0), 1)
        at = turn.astype(jnp.int32) * width + i % width
        picks.append(jnp.where(iota(shape, 1) == at, 1.0, 0.0).astype(jnp.bfloat16))
    every = jnp.dot(
        jnp.concatenate(tokens, axis=0).astype(jnp.bfloat16), maps_ref[...], preferred_element_type=jnp.float32
    )
    slot = jnp.concatenate(slots, axis=0).astype(jnp.int32)
    two = jnp.zeros((here * each, lanes), jnp.float32)
    for pair in range(every.shape[1] // lanes):
        two = jnp.where(slot // 2 == pair, every[:, pair * lanes:(pair + 1) * lanes], two)
    own = jnp.where(slot % 2 == 1, two[:, width:], two[:, :width])
    high = own.astype(jnp.bfloat16).astype(jnp.float32)
    both = jnp.concatenate([high, own - high], axis=1)
    ups = jnp.dot(jnp.concatenate(picks, axis=0), ups_ref[...], preferred_element_type=jnp.float32)
    for k in range(here):
        out_ref[k] = jnp.concatenate(
            [
                both[k * each:(k + 1) * each],
                jnp.zeros((RETURN_ROWS - each, lanes), jnp.float32),
                ups[k * PAIR * width:(k + 1) * PAIR * width],
            ],
            axis=0,
        ).astype(jnp.bfloat16)


def rank_products(rows, maps, ups, steps):
    replicas, count, lanes = rows.shape
    here = 8
    out_rows = RETURN_ROWS + PAIR * lanes // 2
    whole = lambda x: pl.BlockSpec(x.shape, lambda i: (0, 0))
    return pl.pallas_call(
        functools.partial(rank_kernel, steps),
        grid=(replicas // here,),
        in_specs=[pl.BlockSpec((here, count, lanes), lambda i: (i, 0, 0)), whole(maps), whole(ups)],
        out_specs=pl.BlockSpec((here, out_rows, lanes), lambda i: (i, 0, 0)),
        out_shape=jax.ShapeDtypeStruct((replicas, out_rows, lanes), jnp.bfloat16),
        compiler_params=pltpu.CompilerParams(vmem_limit_bytes=60 * 2**20),
        cost_estimate=pl.CostEstimate(flops=2**32, bytes_accessed=8 * 2**20, transcendentals=0),
        name="rank_products",
    )(rows, maps, ups)


def collect_kernel(column_ref, returned_ref, out_ref):
    replicas, rows, lanes = returned_ref.shape
    tokens, width = column_ref.shape[0], lanes // 2
    pick = jnp.where(iota((tokens, replicas * rows), 1) == column_ref[...], 1.0, 0.0).astype(jnp.bfloat16)
    both = jnp.dot(pick, returned_ref[...].reshape(replicas * rows, lanes), preferred_element_type=jnp.float32)
    value = both[:, :width] + both[:, width:]
    out_ref[...] = jnp.concatenate([value[: tokens // 2], value[tokens // 2:]], axis=1)


def collect(column, returned):
    tokens = column.shape[0]
    replicas, _, lanes = returned.shape
    return pl.pallas_call(
        collect_kernel,
        grid=(1,),
        in_specs=[
            pl.BlockSpec((tokens, 1), lambda i: (0, 0)),
            pl.BlockSpec((replicas, RETURN_ROWS, lanes), lambda i: (0, 0, 0)),
        ],
        out_specs=pl.BlockSpec((tokens // 2, lanes), lambda i: (0, 0)),
        out_shape=jax.ShapeDtypeStruct((tokens // 2, lanes), jnp.float32),
        compiler_params=pltpu.CompilerParams(vmem_limit_bytes=24 * 2**20),
        name="collect",
    )(column, returned)


def heads_first(value, heads):
    return jnp.concatenate([value[:, h * HD:(h + 1) * HD] for h in range(heads)], axis=0)


def cached_kernel(steps, bias_ref, queries_ref, keys_ref, values_ref, mixed_ref, weight_ref):
    heads = queries_ref.shape[1] // HD
    rows = keys_ref.shape[0] // GROUP if keys_ref.ndim == 3 else 1
    cache = keys_ref.shape[1]
    count = GROUP * steps
    for g in range(rows):
        query = heads_first(queries_ref[g * count:(g + 1) * count, :], heads)
        keys = keys_ref[g * GROUP:(g + 1) * GROUP].reshape(GROUP * cache, HD)
        values = values_ref[g * GROUP:(g + 1) * GROUP].reshape(GROUP * cache, HD)
        score = lax.dot_general(query, keys, (((1,), (1,)), ((), ())), preferred_element_type=jnp.float32)
        shape = score.shape
        own = (iota(shape, 0) // steps) % GROUP == iota(shape, 1) // cache
        score = jnp.where(own, score * HD ** -0.5 + bias_ref[g], masked_score)
        highest = jnp.max(score, axis=1, keepdims=True)
        exped = jnp.exp(score - highest)
        summed = total(exped, 1)
        mixed = jnp.dot(exped.astype(jnp.bfloat16), values, preferred_element_type=jnp.float32)
        mixed_ref[g] = mixed / summed
        weight_ref[g] = jnp.broadcast_to(highest + jnp.log(summed), mixed.shape)


def cached_attention(lengths, queries, keys, values, steps):
    rows, cache = keys.shape[:2]
    heads = queries.shape[1] // HD
    groups = rows // GROUP
    count = GROUP * steps * heads
    live = jnp.arange(cache, dtype=jnp.int32)[None, :] < lengths[:, None]
    bias = jnp.where(live, 0.0, masked_score).astype(jnp.float32).reshape(groups, 1, GROUP * cache)
    per = 2
    return pl.pallas_call(
        functools.partial(cached_kernel, steps),
        grid=(groups // per,),
        in_specs=[
            pl.BlockSpec((per, 1, GROUP * cache), lambda i: (i, 0, 0)),
            pl.BlockSpec((per * GROUP * steps, heads * HD), lambda i: (i, 0)),
            pl.BlockSpec((per * GROUP, cache, HD), lambda i: (i, 0, 0)),
            pl.BlockSpec((per * GROUP, cache, HD), lambda i: (i, 0, 0)),
        ],
        out_specs=[pl.BlockSpec((per, count, HD), lambda i: (i, 0, 0))] * 2,
        out_shape=[jax.ShapeDtypeStruct((groups, count, HD), jnp.float32)] * 2,
        compiler_params=pltpu.CompilerParams(vmem_limit_bytes=24 * 2**20),
        cost_estimate=pl.CostEstimate(flops=2**31, bytes_accessed=8 * 2**20, transcendentals=2**20),
        name="cached_attention",
    )(bias, queries, keys, values)


def finish_kernel(steps, rank, fetch_ref, a_ref, b_ref, c_ref, d_ref, first_ref, second_ref, base_ref, queries_ref, mixed_ref, weight_ref, fresh_ref, out_ref, held_ref):
    heads = queries_ref.shape[1] // HD
    count = GROUP * steps
    tokens = fetch_ref.shape[0]

    @pl.when(pl.program_id(0) == 0)
    def _():
        summed = (a_ref[...] + b_ref[...]) + (c_ref[...] + d_ref[...])
        width = summed.shape[1] // 2
        low = jnp.concatenate([summed[:, :width], summed[:, width:]], axis=0)
        fetch = fetch_ref[...]
        lanes = iota((tokens, LANES), 1) // rank
        owners = first_ref.shape[0]
        for side in range(2):
            four = jnp.concatenate([low[:, side * rank:(side + 1) * rank]] * (LANES // rank), axis=1)
            delta = jnp.zeros((tokens, HD), jnp.float32)
            for turn, maps_ref in enumerate((first_ref, second_ref)):
                spread = jnp.concatenate(
                    [
                        jnp.where(fetch == PAIR * (lanes + k * (LANES // rank)) + turn, four, 0.0).astype(jnp.bfloat16)
                        for k in range(owners * rank // LANES)
                    ],
                    axis=1,
                )
                maps = maps_ref[:, side * rank:(side + 1) * rank, :].reshape(owners * rank, HD)
                delta += jnp.dot(spread, maps, preferred_element_type=jnp.float32)
            new = base_ref[:, side * HD:(side + 1) * HD] + delta
            held_ref[:, side * HD:(side + 1) * HD] = new.astype(jnp.bfloat16)
        fresh_ref[...] = held_ref[...]

    for g in range(mixed_ref.shape[0]):
        start = pl.multiple_of((pl.program_id(0) * mixed_ref.shape[0] + g) * count, count)
        new = held_ref[pl.ds(start, count), :]
        query = heads_first(queries_ref[g * count:(g + 1) * count, :], heads)
        score = lax.dot_general(
            query, new[:, :HD], (((1,), (1,)), ((), ())), preferred_element_type=jnp.float32
        )
        i, j = iota(score.shape, 0), iota(score.shape, 1)
        seen = ((i // steps) % GROUP == j // steps) & (j % steps <= i % steps)
        score = jnp.where(seen, score * HD ** -0.5, masked_score)
        weight = weight_ref[g]
        highest = jnp.maximum(jnp.max(score, axis=1, keepdims=True), weight)
        exped = jnp.exp(score - highest[:, :count]).astype(jnp.bfloat16)
        cached = jnp.exp(weight - highest)
        ones = jnp.ones((count, HD), jnp.bfloat16)
        both = jnp.dot(
            exped, jnp.concatenate([new[:, HD:], ones], axis=1), preferred_element_type=jnp.float32
        )
        mixed = (mixed_ref[g] * cached + both[:, :HD]) / (cached + both[:, HD:])
        for h in range(heads):
            part = mixed[h * count:(h + 1) * count].reshape(GROUP, steps, HD)
            out_ref[g * GROUP:(g + 1) * GROUP, :, h * HD:(h + 1) * HD] = part.astype(jnp.bfloat16)


def finish(fetch, parts, returned, base, queries, mixed, weight, steps, rank):
    tokens, features = queries.shape
    groups, rows = mixed.shape[:2]
    per = 4
    whole = lambda x: pl.BlockSpec(x.shape, lambda i: (0,) * x.ndim)
    block = pl.BlockSpec((per * GROUP * steps, features), lambda i: (i, 0))
    ups = lambda k: pl.BlockSpec((returned.shape[0], PAIR * rank, HD), lambda i: (0, k, 0))
    return pl.pallas_call(
        functools.partial(finish_kernel, steps, rank),
        grid=(groups // per,),
        in_specs=[whole(fetch)] + [whole(p) for p in parts] + [ups(1), ups(2), whole(base), block]
        + [pl.BlockSpec((per, rows, HD), lambda i: (i, 0, 0))] * 2,
        out_specs=[
            pl.BlockSpec(base.shape, lambda i: (0, 0)),
            pl.BlockSpec((per * GROUP, steps, features), lambda i: (i, 0, 0)),
        ],
        out_shape=[
            jax.ShapeDtypeStruct(base.shape, jnp.bfloat16),
            jax.ShapeDtypeStruct((tokens // steps, steps, features), jnp.bfloat16),
        ],
        scratch_shapes=[pltpu.VMEM(base.shape, jnp.bfloat16)],
        compiler_params=pltpu.CompilerParams(vmem_limit_bytes=32 * 2**20),
        name="finish",
    )(fetch, *parts, returned, returned, base, queries, mixed, weight)


def shifted(value, dx, dy):
    pairs = [(t, ((t // 2 + dx) % 4) * 2 + ((t % 2) ^ dy)) for t in range(8)]
    return lax.ppermute(value, "tensor", pairs)


def project(tokens, key_value_weight):
    half = tokens.shape[0] // 2
    here = lax.axis_index("tensor")
    x, y = here >> 1, here & 1
    depth = tokens.shape[1]

    def product(piece, dx, dy):
        start = ((((x - dx) & 3) << 1) | (y ^ dy)) * depth
        part = lax.dynamic_slice_in_dim(key_value_weight, start, depth, 0)
        return jnp.dot(piece, part.reshape(depth, -1), preferred_element_type=jnp.float32)

    right = shifted(tokens, 1, 0)
    left = shifted(tokens, -1, 0)
    across = shifted(tokens, 0, 1)
    right_across = shifted(across, 1, 0)
    left_across = shifted(across, -1, 0)
    far = jnp.concatenate([shifted(right[:half], 1, 0), shifted(left[half:], -1, 0)], axis=0)
    far_across = shifted(far, 0, 1)
    base = product(tokens, 0, 0) + product(across, 0, 1)
    base = base + product(right, 1, 0) + product(left, -1, 0)
    base = base + product(far, 2, 0) + product(right_across, 1, 1) + product(left_across, -1, 1)
    return base + product(far_across, 2, 1)


def per_device(
    hidden,
    queries,
    key_cache_rows,
    value_cache_rows,
    lengths,
    request_adapter,
    block_first_row,
    adapter_owner_group,
    key_value_weight,
    adapter_down_weight,
    adapter_up_weight,
):
    row_count, steps, depth = hidden.shape
    replicas = lax.axis_size("replica")
    token_count = row_count * steps
    held, sides, rank = adapter_down_weight.shape[:3]
    tokens = hidden.reshape(token_count, depth)

    sent, column, fetch = place(
        block_first_row, request_adapter, adapter_owner_group, tokens, steps, replicas
    )
    received = lax.all_to_all(sent, "replica", split_axis=0, concat_axis=0, tiled=True)

    base = project(tokens, key_value_weight)
    query_tokens = queries.reshape(token_count, -1)
    mixed, weight = cached_attention(lengths, query_tokens, key_cache_rows, value_cache_rows, steps)

    down = adapter_down_weight.reshape(held * sides * rank, depth).T
    received, base, mixed, weight, down = lax.optimization_barrier((received, base, mixed, weight, down))
    products = rank_products(
        received,
        down,
        adapter_up_weight.reshape(held * sides * rank, HD),
        steps,
    )
    returned = lax.all_to_all(products, "replica", split_axis=0, concat_axis=0, tiled=True)
    mine = collect(column, returned)
    mine = mine + shifted(mine, 0, 1)
    parts = (mine, shifted(mine, 2, 0), shifted(mine, 1, 0), shifted(mine, -1, 0))
    fresh, attended = finish(fetch, parts, returned, base, query_tokens, mixed, weight, steps, rank)
    return fresh.reshape(row_count, steps, sides, HD), attended


def solution(mesh):
    placed = (
        P("replica", None, "tensor"),
        P("replica", None, "tensor"),
        P("replica", None, "tensor"),
        P("replica", None, "tensor"),
        P("replica"),
        P("replica"),
        P("replica"),
        P(),
        P(None, None, "tensor"),
        P("replica", None, None, "tensor"),
        P("replica", None, None, "tensor"),
    )
    return jax.shard_map(
        per_device,
        mesh=mesh,
        in_specs=placed,
        out_specs=(P("replica", None, None, "tensor"), P("replica", None, "tensor")),
        check_vma=False,
    )
```

```python
import functools

import jax
import jax.numpy as jnp
from jax import lax
from jax.experimental import pallas as pl
from jax.experimental.pallas import tpu as pltpu
from jax.sharding import PartitionSpec as P

HD = 128
BLK = 7
PAIR = 2
PAIR_ROWS = PAIR * BLK
ASK_ROWS = 8
RETURN_ROWS = 64
LANES = 128
GROUP = 8

masked_score = -1e30


def iota(shape, dim):
    return lax.broadcasted_iota(jnp.int32, shape, dim)


def total(value, axis):
    return jnp.sum(value, axis=axis, keepdims=True)


def place_kernel(steps, first_ref, request_ref, owner_ref, tokens_ref, sent_ref, column_ref, fetch_ref, row_ref, info_ref):
    here, _, lanes = sent_ref.shape
    each = PAIR_ROWS * steps
    token_count, depth = tokens_ref.shape

    @pl.when(pl.program_id(0) == 0)
    def _():
        first = first_ref[...]
        blocks = first.shape[1]
        rows = request_ref.shape[1]
        pool = owner_ref.shape[1]
        owners = owner_ref[...]
        i, j = iota((blocks, blocks), 0), iota((blocks, blocks), 1)

        def down(value):
            return total(jnp.where(i == j, value, 0), 1)

        def across(value):
            return total(jnp.where(i == j, value, 0), 0)

        first_c = down(first)
        after_c = total(jnp.where(j == i + 1, first, 0), 1) + jnp.where(i[:, :1] == blocks - 1, rows, 0)
        after = across(after_c)
        adapter_c = total(jnp.where(iota((blocks, rows), 1) == first_c, request_ref[...], 0), 1)
        ids = iota((blocks, pool), 1)
        owner_c = total(jnp.where(ids == adapter_c, owners, 0), 1)
        slot_c = total(jnp.where((owners == owner_c) & (ids < adapter_c), 1, 0), 1)
        owner, slot = across(owner_c), across(slot_c)
        before = (owner == owner_c) & (j < i)
        turn_c = total(jnp.where(before, 1, 0), 1)
        offset_c = total(jnp.where(before, after - first, 0), 1)
        turn, offset = across(turn_c), across(offset_c)

        r, b = iota((rows, blocks), 0), iota((rows, blocks), 1)
        member = (first <= r) & (r < after)
        spot = r[:, :1] + total(jnp.where(member, offset - first, 0), 1)
        row_slot = total(jnp.where(member, slot, 0), 1)
        r_row = iota((blocks, rows), 1)
        row_owner = total(jnp.where((first_c <= r_row) & (r_row < after_c), owner_c, 0), 0)
        count = info_ref.shape[0]
        goes = jnp.where(iota((count, rows), 0) == row_owner, 1.0, 0.0).astype(jnp.bfloat16)
        asks = jnp.where(iota((rows, lanes), 1) == spot, row_slot, 0).astype(jnp.float32).astype(jnp.bfloat16)
        info = jnp.dot(goes, asks, preferred_element_type=jnp.float32)
        goes = jnp.where(iota((count, blocks), 0) == owner, 1.0, 0.0).astype(jnp.bfloat16)
        asks = jnp.where(iota((blocks, lanes), 1) == PAIR_ROWS + turn_c, slot_c, 0)
        asks = asks.astype(jnp.float32).astype(jnp.bfloat16)
        info_ref[...] = info + jnp.dot(goes, asks, preferred_element_type=jnp.float32)

        t = iota((blocks, token_count), 1)
        member = (first_c * steps <= t) & (t < after_c * steps)
        row_ref[...] = t[:1] + total(
            jnp.where(member, (owner_c * PAIR_ROWS + offset_c - first_c) * steps, 0), 0
        )
        t = iota((token_count, blocks), 0)
        member = (first * steps <= t) & (t < after * steps)
        column_ref[...] = t[:, :1] + total(
            jnp.where(member, owner * RETURN_ROWS + (offset - first) * steps, 0), 1
        )
        fetch_ref[...] = total(jnp.where(member, owner * PAIR + turn, 0), 1)

    spots = iota((here * each, token_count), 0) + pl.program_id(0) * (here * each)
    pick = jnp.where(spots == row_ref[...], 1.0, 0.0).astype(jnp.bfloat16)
    picked = jnp.dot(pick, tokens_ref[...], preferred_element_type=jnp.float32)
    for k in range(here):
        asked = info_ref[pl.ds(pl.program_id(0) * here + k, 1), :]
        parts = [picked[k * each:(k + 1) * each, c * lanes:(c + 1) * lanes] for c in range(depth // lanes)]
        parts.append(jnp.where(iota((ASK_ROWS, lanes), 0) == 0, asked, 0.0))
        sent_ref[k] = jnp.concatenate(parts, axis=0).astype(jnp.bfloat16)


def place(first, request, owners, tokens, steps, replicas):
    token_count, depth = tokens.shape
    rows = PAIR_ROWS * steps * depth // LANES + ASK_ROWS
    here = 4
    whole = lambda shape: pl.BlockSpec(shape, lambda i: (0, 0))
    return pl.pallas_call(
        functools.partial(place_kernel, steps),
        grid=(replicas // here,),
        in_specs=[
            whole((1, first.shape[0])), whole((1, request.shape[0])), whole((1, owners.shape[0])),
            whole((token_count, depth)),
        ],
        out_specs=[
            pl.BlockSpec((here, rows, LANES), lambda i: (i, 0, 0)),
            whole((token_count, 1)), whole((token_count, 1)),
        ],
        out_shape=[
            jax.ShapeDtypeStruct((replicas, rows, LANES), jnp.bfloat16),
            jax.ShapeDtypeStruct((token_count, 1), jnp.int32),
            jax.ShapeDtypeStruct((token_count, 1), jnp.int32),
        ],
        scratch_shapes=[pltpu.VMEM((1, token_count), jnp.int32), pltpu.VMEM((replicas, LANES), jnp.float32)],
        compiler_params=pltpu.CompilerParams(vmem_limit_bytes=24 * 2**20),
        name="place_rows",
    )(first[None], request[None], owners[None], tokens)


def rank_kernel(steps, rows_ref, maps_ref, ups_ref, out_ref):
    here, _, lanes = rows_ref.shape
    each = PAIR_ROWS * steps
    width = lanes // 2
    depth = maps_ref.shape[0]
    tokens, slots, picks = [], [], []
    for k in range(here):
        got = rows_ref[k].astype(jnp.float32)
        chunks = [got[c * each:(c + 1) * each] for c in range(depth // lanes)]
        tokens.append(jnp.concatenate(chunks, axis=1))
        asked = got[each * (depth // lanes):][:1]
        shape = (each, lanes)
        slots.append(total(jnp.where(iota(shape, 1) == iota(shape, 0) // steps, asked, 0.0), 1))
        shape = (PAIR * width, ups_ref.shape[0])
        i = iota((PAIR * width, 1), 0)
        turn = total(jnp.where(iota((PAIR * width, lanes), 1) == PAIR_ROWS + i // width, asked, 0.0), 1)
        at = turn.astype(jnp.int32) * width + i % width
        picks.append(jnp.where(iota(shape, 1) == at, 1.0, 0.0).astype(jnp.bfloat16))
    every = jnp.dot(
        jnp.concatenate(tokens, axis=0).astype(jnp.bfloat16), maps_ref[...], preferred_element_type=jnp.float32
    )
    slot = jnp.concatenate(slots, axis=0).astype(jnp.int32)
    two = jnp.zeros((here * each, lanes), jnp.float32)
    for pair in range(every.shape[1] // lanes):
        two = jnp.where(slot // 2 == pair, every[:, pair * lanes:(pair + 1) * lanes], two)
    own = jnp.where(slot % 2 == 1, two[:, width:], two[:, :width])
    high = own.astype(jnp.bfloat16).astype(jnp.float32)
    both = jnp.concatenate([high, own - high], axis=1)
    ups = jnp.dot(jnp.concatenate(picks, axis=0), ups_ref[...], preferred_element_type=jnp.float32)
    for k in range(here):
        out_ref[k] = jnp.concatenate(
            [
                both[k * each:(k + 1) * each],
                jnp.zeros((RETURN_ROWS - each, lanes), jnp.float32),
                ups[k * PAIR * width:(k + 1) * PAIR * width],
            ],
            axis=0,
        ).astype(jnp.bfloat16)


def rank_products(rows, maps, ups, steps):
    replicas, count, lanes = rows.shape
    here = 8
    out_rows = RETURN_ROWS + PAIR * lanes // 2
    whole = lambda x: pl.BlockSpec(x.shape, lambda i: (0, 0))
    return pl.pallas_call(
        functools.partial(rank_kernel, steps),
        grid=(replicas // here,),
        in_specs=[pl.BlockSpec((here, count, lanes), lambda i: (i, 0, 0)), whole(maps), whole(ups)],
        out_specs=pl.BlockSpec((here, out_rows, lanes), lambda i: (i, 0, 0)),
        out_shape=jax.ShapeDtypeStruct((replicas, out_rows, lanes), jnp.bfloat16),
        compiler_params=pltpu.CompilerParams(vmem_limit_bytes=60 * 2**20),
        cost_estimate=pl.CostEstimate(flops=2**32, bytes_accessed=8 * 2**20, transcendentals=0),
        name="rank_products",
    )(rows, maps, ups)


def collect_kernel(column_ref, returned_ref, out_ref):
    replicas, rows, lanes = returned_ref.shape
    tokens, width = column_ref.shape[0], lanes // 2
    pick = jnp.where(iota((tokens, replicas * rows), 1) == column_ref[...], 1.0, 0.0).astype(jnp.bfloat16)
    both = jnp.dot(pick, returned_ref[...].reshape(replicas * rows, lanes), preferred_element_type=jnp.float32)
    value = both[:, :width] + both[:, width:]
    out_ref[...] = jnp.concatenate([value[: tokens // 2], value[tokens // 2:]], axis=1)


def collect(column, returned):
    tokens = column.shape[0]
    replicas, _, lanes = returned.shape
    return pl.pallas_call(
        collect_kernel,
        grid=(1,),
        in_specs=[
            pl.BlockSpec((tokens, 1), lambda i: (0, 0)),
            pl.BlockSpec((replicas, RETURN_ROWS, lanes), lambda i: (0, 0, 0)),
        ],
        out_specs=pl.BlockSpec((tokens // 2, lanes), lambda i: (0, 0)),
        out_shape=jax.ShapeDtypeStruct((tokens // 2, lanes), jnp.float32),
        compiler_params=pltpu.CompilerParams(vmem_limit_bytes=24 * 2**20),
        name="collect",
    )(column, returned)


def heads_first(value, heads):
    return jnp.concatenate([value[:, h * HD:(h + 1) * HD] for h in range(heads)], axis=0)


def cached_kernel(steps, bias_ref, queries_ref, keys_ref, values_ref, mixed_ref, weight_ref):
    heads = queries_ref.shape[1] // HD
    rows = keys_ref.shape[0] // GROUP if keys_ref.ndim == 3 else 1
    cache = keys_ref.shape[1]
    count = GROUP * steps
    for g in range(rows):
        query = heads_first(queries_ref[g * count:(g + 1) * count, :], heads)
        keys = keys_ref[g * GROUP:(g + 1) * GROUP].reshape(GROUP * cache, HD)
        values = values_ref[g * GROUP:(g + 1) * GROUP].reshape(GROUP * cache, HD)
        score = lax.dot_general(query, keys, (((1,), (1,)), ((), ())), preferred_element_type=jnp.float32)
        shape = score.shape
        own = (iota(shape, 0) // steps) % GROUP == iota(shape, 1) // cache
        score = jnp.where(own, score * HD ** -0.5 + bias_ref[g], masked_score)
        highest = jnp.max(score, axis=1, keepdims=True)
        exped = jnp.exp(score - highest)
        summed = total(exped, 1)
        mixed = jnp.dot(exped.astype(jnp.bfloat16), values, preferred_element_type=jnp.float32)
        mixed_ref[g] = mixed / summed
        weight_ref[g] = jnp.broadcast_to(highest + jnp.log(summed), mixed.shape)


def cached_attention(lengths, queries, keys, values, steps):
    rows, cache = keys.shape[:2]
    heads = queries.shape[1] // HD
    groups = rows // GROUP
    count = GROUP * steps * heads
    live = jnp.arange(cache, dtype=jnp.int32)[None, :] < lengths[:, None]
    bias = jnp.where(live, 0.0, masked_score).astype(jnp.float32).reshape(groups, 1, GROUP * cache)
    per = 2
    return pl.pallas_call(
        functools.partial(cached_kernel, steps),
        grid=(groups // per,),
        in_specs=[
            pl.BlockSpec((per, 1, GROUP * cache), lambda i: (i, 0, 0)),
            pl.BlockSpec((per * GROUP * steps, heads * HD), lambda i: (i, 0)),
            pl.BlockSpec((per * GROUP, cache, HD), lambda i: (i, 0, 0)),
            pl.BlockSpec((per * GROUP, cache, HD), lambda i: (i, 0, 0)),
        ],
        out_specs=[pl.BlockSpec((per, count, HD), lambda i: (i, 0, 0))] * 2,
        out_shape=[jax.ShapeDtypeStruct((groups, count, HD), jnp.float32)] * 2,
        compiler_params=pltpu.CompilerParams(vmem_limit_bytes=24 * 2**20),
        cost_estimate=pl.CostEstimate(flops=2**31, bytes_accessed=8 * 2**20, transcendentals=2**20),
        name="cached_attention",
    )(bias, queries, keys, values)


def finish_kernel(steps, rank, fetch_ref, a_ref, b_ref, c_ref, d_ref, first_ref, second_ref, base_ref, queries_ref, mixed_ref, weight_ref, fresh_ref, out_ref, held_ref):
    heads = queries_ref.shape[1] // HD
    count = GROUP * steps
    tokens = fetch_ref.shape[0]

    @pl.when(pl.program_id(0) == 0)
    def _():
        summed = (a_ref[...] + b_ref[...]) + (c_ref[...] + d_ref[...])
        width = summed.shape[1] // 2
        low = jnp.concatenate([summed[:, :width], summed[:, width:]], axis=0)
        fetch = fetch_ref[...]
        lanes = iota((tokens, LANES), 1) // rank
        owners = first_ref.shape[0]
        for side in range(2):
            four = jnp.concatenate([low[:, side * rank:(side + 1) * rank]] * (LANES // rank), axis=1)
            delta = jnp.zeros((tokens, HD), jnp.float32)
            for turn, maps_ref in enumerate((first_ref, second_ref)):
                spread = jnp.concatenate(
                    [
                        jnp.where(fetch == PAIR * (lanes + k * (LANES // rank)) + turn, four, 0.0).astype(jnp.bfloat16)
                        for k in range(owners * rank // LANES)
                    ],
                    axis=1,
                )
                maps = maps_ref[:, side * rank:(side + 1) * rank, :].reshape(owners * rank, HD)
                delta += jnp.dot(spread, maps, preferred_element_type=jnp.float32)
            new = base_ref[:, side * HD:(side + 1) * HD] + delta
            held_ref[:, side * HD:(side + 1) * HD] = new.astype(jnp.bfloat16)
        fresh_ref[...] = held_ref[...]

    for g in range(mixed_ref.shape[0]):
        start = pl.multiple_of((pl.program_id(0) * mixed_ref.shape[0] + g) * count, count)
        new = held_ref[pl.ds(start, count), :]
        query = heads_first(queries_ref[g * count:(g + 1) * count, :], heads)
        score = lax.dot_general(
            query, new[:, :HD], (((1,), (1,)), ((), ())), preferred_element_type=jnp.float32
        )
        i, j = iota(score.shape, 0), iota(score.shape, 1)
        seen = ((i // steps) % GROUP == j // steps) & (j % steps <= i % steps)
        score = jnp.where(seen, score * HD ** -0.5, masked_score)
        weight = weight_ref[g]
        highest = jnp.maximum(jnp.max(score, axis=1, keepdims=True), weight)
        exped = jnp.exp(score - highest[:, :count]).astype(jnp.bfloat16)
        cached = jnp.exp(weight - highest)
        ones = jnp.ones((count, HD), jnp.bfloat16)
        both = jnp.dot(
            exped, jnp.concatenate([new[:, HD:], ones], axis=1), preferred_element_type=jnp.float32
        )
        mixed = (mixed_ref[g] * cached + both[:, :HD]) / (cached + both[:, HD:])
        for h in range(heads):
            part = mixed[h * count:(h + 1) * count].reshape(GROUP, steps, HD)
            out_ref[g * GROUP:(g + 1) * GROUP, :, h * HD:(h + 1) * HD] = part.astype(jnp.bfloat16)


def finish(fetch, parts, returned, base, queries, mixed, weight, steps, rank):
    tokens, features = queries.shape
    groups, rows = mixed.shape[:2]
    per = 4
    whole = lambda x: pl.BlockSpec(x.shape, lambda i: (0,) * x.ndim)
    block = pl.BlockSpec((per * GROUP * steps, features), lambda i: (i, 0))
    ups = lambda k: pl.BlockSpec((returned.shape[0], PAIR * rank, HD), lambda i: (0, k, 0))
    return pl.pallas_call(
        functools.partial(finish_kernel, steps, rank),
        grid=(groups // per,),
        in_specs=[whole(fetch)] + [whole(p) for p in parts] + [ups(1), ups(2), whole(base), block]
        + [pl.BlockSpec((per, rows, HD), lambda i: (i, 0, 0))] * 2,
        out_specs=[
            pl.BlockSpec(base.shape, lambda i: (0, 0)),
            pl.BlockSpec((per * GROUP, steps, features), lambda i: (i, 0, 0)),
        ],
        out_shape=[
            jax.ShapeDtypeStruct(base.shape, jnp.bfloat16),
            jax.ShapeDtypeStruct((tokens // steps, steps, features), jnp.bfloat16),
        ],
        scratch_shapes=[pltpu.VMEM(base.shape, jnp.bfloat16)],
        compiler_params=pltpu.CompilerParams(vmem_limit_bytes=32 * 2**20),
        name="finish",
    )(fetch, *parts, returned, returned, base, queries, mixed, weight)


def shifted(value, dx, dy):
    pairs = [(t, ((t // 2 + dx) % 4) * 2 + ((t % 2) ^ dy)) for t in range(8)]
    return lax.ppermute(value, "tensor", pairs)


def project(tokens, key_value_weight):
    half = tokens.shape[0] // 2
    here = lax.axis_index("tensor")
    x, y = here >> 1, here & 1
    depth = tokens.shape[1]

    def product(piece, dx, dy):
        start = ((((x - dx) & 3) << 1) | (y ^ dy)) * depth
        part = lax.dynamic_slice_in_dim(key_value_weight, start, depth, 0)
        return jnp.dot(piece, part.reshape(depth, -1), preferred_element_type=jnp.float32)

    right = shifted(tokens, 1, 0)
    left = shifted(tokens, -1, 0)
    across = shifted(tokens, 0, 1)
    right_across = shifted(across, 1, 0)
    left_across = shifted(across, -1, 0)
    far = jnp.concatenate([shifted(right[:half], 1, 0), shifted(left[half:], -1, 0)], axis=0)
    far_across = shifted(far, 0, 1)
    base = product(tokens, 0, 0) + product(across, 0, 1)
    base = base + product(right, 1, 0) + product(left, -1, 0)
    base = base + product(far, 2, 0) + product(right_across, 1, 1) + product(left_across, -1, 1)
    return base, lambda: product(far_across, 2, 1)


def per_device(
    hidden,
    queries,
    key_cache_rows,
    value_cache_rows,
    lengths,
    request_adapter,
    block_first_row,
    adapter_owner_group,
    key_value_weight,
    adapter_down_weight,
    adapter_up_weight,
):
    row_count, steps, depth = hidden.shape
    replicas = lax.axis_size("replica")
    token_count = row_count * steps
    held, sides, rank = adapter_down_weight.shape[:3]
    tokens = hidden.reshape(token_count, depth)

    sent, column, fetch = place(
        block_first_row, request_adapter, adapter_owner_group, tokens, steps, replicas
    )
    received = lax.all_to_all(sent, "replica", split_axis=0, concat_axis=0, tiled=True)

    near, last = project(tokens, key_value_weight)
    query_tokens = queries.reshape(token_count, -1)
    mixed, weight = cached_attention(lengths, query_tokens, key_cache_rows, value_cache_rows, steps)

    down = adapter_down_weight.reshape(held * sides * rank, depth).T
    received, near, mixed, weight, down = lax.optimization_barrier((received, near, mixed, weight, down))
    products = rank_products(
        received,
        down,
        adapter_up_weight.reshape(held * sides * rank, HD),
        steps,
    )
    returned = lax.all_to_all(products, "replica", split_axis=0, concat_axis=0, tiled=True)
    mine = collect(column, returned)
    mine = mine + shifted(mine, 0, 1)
    parts = (mine, shifted(mine, 2, 0), shifted(mine, 1, 0), shifted(mine, -1, 0))
    fresh, attended = finish(fetch, parts, returned, near + last(), query_tokens, mixed, weight, steps, rank)
    return fresh.reshape(row_count, steps, sides, HD), attended


def solution(mesh):
    placed = (
        P("replica", None, "tensor"),
        P("replica", None, "tensor"),
        P("replica", None, "tensor"),
        P("replica", None, "tensor"),
        P("replica"),
        P("replica"),
        P("replica"),
        P(),
        P(None, None, "tensor"),
        P("replica", None, None, "tensor"),
        P("replica", None, None, "tensor"),
    )
    return jax.shard_map(
        per_device,
        mesh=mesh,
        in_specs=placed,
        out_specs=(P("replica", None, None, "tensor"), P("replica", None, "tensor")),
        check_vma=False,
    )
```

```python
import functools

import jax
import jax.numpy as jnp
from jax import lax
from jax.experimental import pallas as pl
from jax.experimental.pallas import tpu as pltpu
from jax.sharding import PartitionSpec as P

HD = 128
BLK = 7
PAIR = 2
PAIR_ROWS = PAIR * BLK
ASK_ROWS = 8
RETURN_ROWS = 64
LANES = 128
GROUP = 8

masked_score = -1e30


def iota(shape, dim):
    return lax.broadcasted_iota(jnp.int32, shape, dim)


def total(value, axis):
    return jnp.sum(value, axis=axis, keepdims=True)


def place_kernel(steps, first_ref, request_ref, owner_ref, tokens_ref, sent_ref, column_ref, fetch_ref, row_ref, info_ref):
    here, _, lanes = sent_ref.shape
    each = PAIR_ROWS * steps
    token_count, depth = tokens_ref.shape

    @pl.when(pl.program_id(0) == 0)
    def _():
        first = first_ref[...]
        blocks = first.shape[1]
        rows = request_ref.shape[1]
        pool = owner_ref.shape[1]
        owners = owner_ref[...]
        i, j = iota((blocks, blocks), 0), iota((blocks, blocks), 1)

        def down(value):
            return total(jnp.where(i == j, value, 0), 1)

        def across(value):
            return total(jnp.where(i == j, value, 0), 0)

        first_c = down(first)
        after_c = total(jnp.where(j == i + 1, first, 0), 1) + jnp.where(i[:, :1] == blocks - 1, rows, 0)
        after = across(after_c)
        adapter_c = total(jnp.where(iota((blocks, rows), 1) == first_c, request_ref[...], 0), 1)
        ids = iota((blocks, pool), 1)
        owner_c = total(jnp.where(ids == adapter_c, owners, 0), 1)
        slot_c = total(jnp.where((owners == owner_c) & (ids < adapter_c), 1, 0), 1)
        owner, slot = across(owner_c), across(slot_c)
        before = (owner == owner_c) & (j < i)
        turn_c = total(jnp.where(before, 1, 0), 1)
        offset_c = total(jnp.where(before, after - first, 0), 1)
        turn, offset = across(turn_c), across(offset_c)

        r, b = iota((rows, blocks), 0), iota((rows, blocks), 1)
        member = (first <= r) & (r < after)
        spot = r[:, :1] + total(jnp.where(member, offset - first, 0), 1)
        row_slot = total(jnp.where(member, slot, 0), 1)
        r_row = iota((blocks, rows), 1)
        row_owner = total(jnp.where((first_c <= r_row) & (r_row < after_c), owner_c, 0), 0)
        count = info_ref.shape[0]
        goes = jnp.where(iota((count, rows), 0) == row_owner, 1.0, 0.0).astype(jnp.bfloat16)
        asks = jnp.where(iota((rows, lanes), 1) == spot, row_slot, 0).astype(jnp.float32).astype(jnp.bfloat16)
        info = jnp.dot(goes, asks, preferred_element_type=jnp.float32)
        goes = jnp.where(iota((count, blocks), 0) == owner, 1.0, 0.0).astype(jnp.bfloat16)
        asks = jnp.where(iota((blocks, lanes), 1) == PAIR_ROWS + turn_c, slot_c, 0)
        asks = asks.astype(jnp.float32).astype(jnp.bfloat16)
        info_ref[...] = info + jnp.dot(goes, asks, preferred_element_type=jnp.float32)

        t = iota((blocks, token_count), 1)
        member = (first_c * steps <= t) & (t < after_c * steps)
        row_ref[...] = t[:1] + total(
            jnp.where(member, (owner_c * PAIR_ROWS + offset_c - first_c) * steps, 0), 0
        )
        t = iota((token_count, blocks), 0)
        member = (first * steps <= t) & (t < after * steps)
        column_ref[...] = t[:, :1] + total(
            jnp.where(member, owner * RETURN_ROWS + (offset - first) * steps, 0), 1
        )
        fetch_ref[...] = total(jnp.where(member, owner * PAIR + turn, 0), 1)

    spots = iota((here * each, token_count), 0) + pl.program_id(0) * (here * each)
    pick = jnp.where(spots == row_ref[...], 1.0, 0.0).astype(jnp.bfloat16)
    picked = jnp.dot(pick, tokens_ref[...], preferred_element_type=jnp.float32)
    for k in range(here):
        asked = info_ref[pl.ds(pl.program_id(0) * here + k, 1), :]
        parts = [picked[k * each:(k + 1) * each, c * lanes:(c + 1) * lanes] for c in range(depth // lanes)]
        parts.append(jnp.where(iota((ASK_ROWS, lanes), 0) == 0, asked, 0.0))
        sent_ref[k] = jnp.concatenate(parts, axis=0).astype(jnp.bfloat16)


def place(first, request, owners, tokens, steps, replicas):
    token_count, depth = tokens.shape
    rows = PAIR_ROWS * steps * depth // LANES + ASK_ROWS
    here = 8
    whole = lambda shape: pl.BlockSpec(shape, lambda i: (0, 0))
    return pl.pallas_call(
        functools.partial(place_kernel, steps),
        grid=(replicas // here,),
        in_specs=[
            whole((1, first.shape[0])), whole((1, request.shape[0])), whole((1, owners.shape[0])),
            whole((token_count, depth)),
        ],
        out_specs=[
            pl.BlockSpec((here, rows, LANES), lambda i: (i, 0, 0)),
            whole((token_count, 1)), whole((token_count, 1)),
        ],
        out_shape=[
            jax.ShapeDtypeStruct((replicas, rows, LANES), jnp.bfloat16),
            jax.ShapeDtypeStruct((token_count, 1), jnp.int32),
            jax.ShapeDtypeStruct((token_count, 1), jnp.int32),
        ],
        scratch_shapes=[pltpu.VMEM((1, token_count), jnp.int32), pltpu.VMEM((replicas, LANES), jnp.float32)],
        compiler_params=pltpu.CompilerParams(vmem_limit_bytes=24 * 2**20),
        name="place_rows",
    )(first[None], request[None], owners[None], tokens)


def rank_kernel(steps, rows_ref, maps_ref, ups_ref, out_ref):
    here, _, lanes = rows_ref.shape
    each = PAIR_ROWS * steps
    width = lanes // 2
    depth = maps_ref.shape[0]
    tokens, slots, picks = [], [], []
    for k in range(here):
        got = rows_ref[k].astype(jnp.float32)
        chunks = [got[c * each:(c + 1) * each] for c in range(depth // lanes)]
        tokens.append(jnp.concatenate(chunks, axis=1))
        asked = got[each * (depth // lanes):][:1]
        shape = (each, lanes)
        slots.append(total(jnp.where(iota(shape, 1) == iota(shape, 0) // steps, asked, 0.0), 1))
        shape = (PAIR * width, ups_ref.shape[0])
        i = iota((PAIR * width, 1), 0)
        turn = total(jnp.where(iota((PAIR * width, lanes), 1) == PAIR_ROWS + i // width, asked, 0.0), 1)
        at = turn.astype(jnp.int32) * width + i % width
        picks.append(jnp.where(iota(shape, 1) == at, 1.0, 0.0).astype(jnp.bfloat16))
    every = jnp.dot(
        jnp.concatenate(tokens, axis=0).astype(jnp.bfloat16), maps_ref[...], preferred_element_type=jnp.float32
    )
    slot = jnp.concatenate(slots, axis=0).astype(jnp.int32)
    two = jnp.zeros((here * each, lanes), jnp.float32)
    for pair in range(every.shape[1] // lanes):
        two = jnp.where(slot // 2 == pair, every[:, pair * lanes:(pair + 1) * lanes], two)
    own = jnp.where(slot % 2 == 1, two[:, width:], two[:, :width])
    high = own.astype(jnp.bfloat16).astype(jnp.float32)
    both = jnp.concatenate([high, own - high], axis=1)
    ups = jnp.dot(jnp.concatenate(picks, axis=0), ups_ref[...], preferred_element_type=jnp.float32)
    for k in range(here):
        out_ref[k] = jnp.concatenate(
            [
                both[k * each:(k + 1) * each],
                jnp.zeros((RETURN_ROWS - each, lanes), jnp.float32),
                ups[k * PAIR * width:(k + 1) * PAIR * width],
            ],
            axis=0,
        ).astype(jnp.bfloat16)


def rank_products(rows, maps, ups, steps):
    replicas, count, lanes = rows.shape
    here = 8
    out_rows = RETURN_ROWS + PAIR * lanes // 2
    whole = lambda x: pl.BlockSpec(x.shape, lambda i: (0, 0))
    return pl.pallas_call(
        functools.partial(rank_kernel, steps),
        grid=(replicas // here,),
        in_specs=[pl.BlockSpec((here, count, lanes), lambda i: (i, 0, 0)), whole(maps), whole(ups)],
        out_specs=pl.BlockSpec((here, out_rows, lanes), lambda i: (i, 0, 0)),
        out_shape=jax.ShapeDtypeStruct((replicas, out_rows, lanes), jnp.bfloat16),
        compiler_params=pltpu.CompilerParams(vmem_limit_bytes=60 * 2**20),
        cost_estimate=pl.CostEstimate(flops=2**32, bytes_accessed=8 * 2**20, transcendentals=0),
        name="rank_products",
    )(rows, maps, ups)


def collect_kernel(column_ref, returned_ref, out_ref):
    replicas, rows, lanes = returned_ref.shape
    tokens, width = column_ref.shape[0], lanes // 2
    pick = jnp.where(iota((tokens, replicas * rows), 1) == column_ref[...], 1.0, 0.0).astype(jnp.bfloat16)
    both = jnp.dot(pick, returned_ref[...].reshape(replicas * rows, lanes), preferred_element_type=jnp.float32)
    value = both[:, :width] + both[:, width:]
    out_ref[...] = jnp.concatenate([value[: tokens // 2], value[tokens // 2:]], axis=1)


def collect(column, returned):
    tokens = column.shape[0]
    replicas, _, lanes = returned.shape
    return pl.pallas_call(
        collect_kernel,
        grid=(1,),
        in_specs=[
            pl.BlockSpec((tokens, 1), lambda i: (0, 0)),
            pl.BlockSpec((replicas, RETURN_ROWS, lanes), lambda i: (0, 0, 0)),
        ],
        out_specs=pl.BlockSpec((tokens // 2, lanes), lambda i: (0, 0)),
        out_shape=jax.ShapeDtypeStruct((tokens // 2, lanes), jnp.float32),
        compiler_params=pltpu.CompilerParams(vmem_limit_bytes=24 * 2**20),
        name="collect",
    )(column, returned)


def heads_first(value, heads):
    return jnp.concatenate([value[:, h * HD:(h + 1) * HD] for h in range(heads)], axis=0)


def cached_kernel(steps, bias_ref, queries_ref, keys_ref, values_ref, mixed_ref, weight_ref):
    heads = queries_ref.shape[1] // HD
    rows = keys_ref.shape[0] // GROUP if keys_ref.ndim == 3 else 1
    cache = keys_ref.shape[1]
    count = GROUP * steps
    for g in range(rows):
        query = heads_first(queries_ref[g * count:(g + 1) * count, :], heads)
        keys = keys_ref[g * GROUP:(g + 1) * GROUP].reshape(GROUP * cache, HD)
        values = values_ref[g * GROUP:(g + 1) * GROUP].reshape(GROUP * cache, HD)
        score = lax.dot_general(query, keys, (((1,), (1,)), ((), ())), preferred_element_type=jnp.float32)
        shape = score.shape
        own = (iota(shape, 0) // steps) % GROUP == iota(shape, 1) // cache
        score = jnp.where(own, score * HD ** -0.5 + bias_ref[g], masked_score)
        highest = jnp.max(score, axis=1, keepdims=True)
        exped = jnp.exp(score - highest)
        summed = total(exped, 1)
        mixed = jnp.dot(exped.astype(jnp.bfloat16), values, preferred_element_type=jnp.float32)
        mixed_ref[g] = mixed / summed
        weight_ref[g] = jnp.broadcast_to(highest + jnp.log(summed), mixed.shape)


def cached_attention(lengths, queries, keys, values, steps):
    rows, cache = keys.shape[:2]
    heads = queries.shape[1] // HD
    groups = rows // GROUP
    count = GROUP * steps * heads
    live = jnp.arange(cache, dtype=jnp.int32)[None, :] < lengths[:, None]
    bias = jnp.where(live, 0.0, masked_score).astype(jnp.float32).reshape(groups, 1, GROUP * cache)
    per = 2
    return pl.pallas_call(
        functools.partial(cached_kernel, steps),
        grid=(groups // per,),
        in_specs=[
            pl.BlockSpec((per, 1, GROUP * cache), lambda i: (i, 0, 0)),
            pl.BlockSpec((per * GROUP * steps, heads * HD), lambda i: (i, 0)),
            pl.BlockSpec((per * GROUP, cache, HD), lambda i: (i, 0, 0)),
            pl.BlockSpec((per * GROUP, cache, HD), lambda i: (i, 0, 0)),
        ],
        out_specs=[pl.BlockSpec((per, count, HD), lambda i: (i, 0, 0))] * 2,
        out_shape=[jax.ShapeDtypeStruct((groups, count, HD), jnp.float32)] * 2,
        compiler_params=pltpu.CompilerParams(vmem_limit_bytes=24 * 2**20),
        cost_estimate=pl.CostEstimate(flops=2**31, bytes_accessed=8 * 2**20, transcendentals=2**20),
        name="cached_attention",
    )(bias, queries, keys, values)


def finish_kernel(steps, rank, fetch_ref, a_ref, b_ref, c_ref, d_ref, first_ref, second_ref, base_ref, queries_ref, mixed_ref, weight_ref, fresh_ref, out_ref, held_ref):
    heads = queries_ref.shape[1] // HD
    count = GROUP * steps
    tokens = fetch_ref.shape[0]

    @pl.when(pl.program_id(0) == 0)
    def _():
        summed = (a_ref[...] + b_ref[...]) + (c_ref[...] + d_ref[...])
        width = summed.shape[1] // 2
        low = jnp.concatenate([summed[:, :width], summed[:, width:]], axis=0)
        fetch = fetch_ref[...]
        lanes = iota((tokens, LANES), 1) // rank
        owners = first_ref.shape[0]
        for side in range(2):
            four = jnp.concatenate([low[:, side * rank:(side + 1) * rank]] * (LANES // rank), axis=1)
            delta = jnp.zeros((tokens, HD), jnp.float32)
            for turn, maps_ref in enumerate((first_ref, second_ref)):
                spread = jnp.concatenate(
                    [
                        jnp.where(fetch == PAIR * (lanes + k * (LANES // rank)) + turn, four, 0.0).astype(jnp.bfloat16)
                        for k in range(owners * rank // LANES)
                    ],
                    axis=1,
                )
                maps = maps_ref[:, side * rank:(side + 1) * rank, :].reshape(owners * rank, HD)
                delta += jnp.dot(spread, maps, preferred_element_type=jnp.float32)
            new = base_ref[:, side * HD:(side + 1) * HD] + delta
            held_ref[:, side * HD:(side + 1) * HD] = new.astype(jnp.bfloat16)
        fresh_ref[...] = held_ref[...]

    for g in range(mixed_ref.shape[0]):
        start = pl.multiple_of((pl.program_id(0) * mixed_ref.shape[0] + g) * count, count)
        new = held_ref[pl.ds(start, count), :]
        query = heads_first(queries_ref[g * count:(g + 1) * count, :], heads)
        score = lax.dot_general(
            query, new[:, :HD], (((1,), (1,)), ((), ())), preferred_element_type=jnp.float32
        )
        i, j = iota(score.shape, 0), iota(score.shape, 1)
        seen = ((i // steps) % GROUP == j // steps) & (j % steps <= i % steps)
        score = jnp.where(seen, score * HD ** -0.5, masked_score)
        weight = weight_ref[g]
        highest = jnp.maximum(jnp.max(score, axis=1, keepdims=True), weight)
        exped = jnp.exp(score - highest[:, :count]).astype(jnp.bfloat16)
        cached = jnp.exp(weight - highest)
        ones = jnp.ones((count, HD), jnp.bfloat16)
        both = jnp.dot(
            exped, jnp.concatenate([new[:, HD:], ones], axis=1), preferred_element_type=jnp.float32
        )
        mixed = (mixed_ref[g] * cached + both[:, :HD]) / (cached + both[:, HD:])
        for h in range(heads):
            part = mixed[h * count:(h + 1) * count].reshape(GROUP, steps, HD)
            out_ref[g * GROUP:(g + 1) * GROUP, :, h * HD:(h + 1) * HD] = part.astype(jnp.bfloat16)


def finish(fetch, parts, returned, base, queries, mixed, weight, steps, rank):
    tokens, features = queries.shape
    groups, rows = mixed.shape[:2]
    per = 4
    whole = lambda x: pl.BlockSpec(x.shape, lambda i: (0,) * x.ndim)
    block = pl.BlockSpec((per * GROUP * steps, features), lambda i: (i, 0))
    ups = lambda k: pl.BlockSpec((returned.shape[0], PAIR * rank, HD), lambda i: (0, k, 0))
    return pl.pallas_call(
        functools.partial(finish_kernel, steps, rank),
        grid=(groups // per,),
        in_specs=[whole(fetch)] + [whole(p) for p in parts] + [ups(1), ups(2), whole(base), block]
        + [pl.BlockSpec((per, rows, HD), lambda i: (i, 0, 0))] * 2,
        out_specs=[
            pl.BlockSpec(base.shape, lambda i: (0, 0)),
            pl.BlockSpec((per * GROUP, steps, features), lambda i: (i, 0, 0)),
        ],
        out_shape=[
            jax.ShapeDtypeStruct(base.shape, jnp.bfloat16),
            jax.ShapeDtypeStruct((tokens // steps, steps, features), jnp.bfloat16),
        ],
        scratch_shapes=[pltpu.VMEM(base.shape, jnp.bfloat16)],
        compiler_params=pltpu.CompilerParams(vmem_limit_bytes=32 * 2**20),
        name="finish",
    )(fetch, *parts, returned, returned, base, queries, mixed, weight)


def shifted(value, dx, dy):
    pairs = [(t, ((t // 2 + dx) % 4) * 2 + ((t % 2) ^ dy)) for t in range(8)]
    return lax.ppermute(value, "tensor", pairs)


def project(tokens, key_value_weight):
    half = tokens.shape[0] // 2
    here = lax.axis_index("tensor")
    x, y = here >> 1, here & 1
    depth = tokens.shape[1]

    def product(piece, dx, dy):
        start = ((((x - dx) & 3) << 1) | (y ^ dy)) * depth
        part = lax.dynamic_slice_in_dim(key_value_weight, start, depth, 0)
        return jnp.dot(piece, part.reshape(depth, -1), preferred_element_type=jnp.float32)

    right = shifted(tokens, 1, 0)
    left = shifted(tokens, -1, 0)
    across = shifted(tokens, 0, 1)
    right_across = shifted(across, 1, 0)
    left_across = shifted(across, -1, 0)
    far = jnp.concatenate([shifted(right[:half], 1, 0), shifted(left[half:], -1, 0)], axis=0)
    far_across = shifted(far, 0, 1)
    base = product(tokens, 0, 0) + product(across, 0, 1)
    base = base + product(right, 1, 0) + product(left, -1, 0)
    base = base + product(far, 2, 0)
    return base, lambda: product(right_across, 1, 1) + product(left_across, -1, 1) + product(far_across, 2, 1)


def per_device(
    hidden,
    queries,
    key_cache_rows,
    value_cache_rows,
    lengths,
    request_adapter,
    block_first_row,
    adapter_owner_group,
    key_value_weight,
    adapter_down_weight,
    adapter_up_weight,
):
    row_count, steps, depth = hidden.shape
    replicas = lax.axis_size("replica")
    token_count = row_count * steps
    held, sides, rank = adapter_down_weight.shape[:3]
    tokens = hidden.reshape(token_count, depth)

    sent, column, fetch = place(
        block_first_row, request_adapter, adapter_owner_group, tokens, steps, replicas
    )
    received = lax.all_to_all(sent, "replica", split_axis=0, concat_axis=0, tiled=True)

    near, last = project(tokens, key_value_weight)
    query_tokens = queries.reshape(token_count, -1)
    mixed, weight = cached_attention(lengths, query_tokens, key_cache_rows, value_cache_rows, steps)

    down = adapter_down_weight.reshape(held * sides * rank, depth).T
    received, near, mixed, weight, down = lax.optimization_barrier((received, near, mixed, weight, down))
    products = rank_products(
        received,
        down,
        adapter_up_weight.reshape(held * sides * rank, HD),
        steps,
    )
    returned = lax.all_to_all(products, "replica", split_axis=0, concat_axis=0, tiled=True)
    mine = collect(column, returned)
    mine = mine + shifted(mine, 0, 1)
    parts = (mine, shifted(mine, 2, 0), shifted(mine, 1, 0), shifted(mine, -1, 0))
    fresh, attended = finish(fetch, parts, returned, near + last(), query_tokens, mixed, weight, steps, rank)
    return fresh.reshape(row_count, steps, sides, HD), attended


def solution(mesh):
    placed = (
        P("replica", None, "tensor"),
        P("replica", None, "tensor"),
        P("replica", None, "tensor"),
        P("replica", None, "tensor"),
        P("replica"),
        P("replica"),
        P("replica"),
        P(),
        P(None, None, "tensor"),
        P("replica", None, None, "tensor"),
        P("replica", None, None, "tensor"),
    )
    return jax.shard_map(
        per_device,
        mesh=mesh,
        in_specs=placed,
        out_specs=(P("replica", None, None, "tensor"), P("replica", None, "tensor")),
        check_vma=False,
    )
```

```python
import functools

import jax
import jax.numpy as jnp
from jax import lax
from jax.experimental import pallas as pl
from jax.experimental.pallas import tpu as pltpu
from jax.sharding import PartitionSpec as P

HD = 128
BLK = 7
PAIR = 2
PAIR_ROWS = PAIR * BLK
ASK_ROWS = 8
LANES = 128
GROUP = 8

masked_score = -1e30


def iota(shape, dim):
    return lax.broadcasted_iota(jnp.int32, shape, dim)


def total(value, axis):
    return jnp.sum(value, axis=axis, keepdims=True)


def place_kernel(steps, first_ref, request_ref, owner_ref, tokens_ref, sent_ref, column_ref, fetch_ref, row_ref, info_ref):
    here, _, lanes = sent_ref.shape
    each = PAIR_ROWS * steps
    token_count, depth = tokens_ref.shape

    @pl.when(pl.program_id(0) == 0)
    def _():
        first = first_ref[...]
        blocks = first.shape[1]
        rows = request_ref.shape[1]
        pool = owner_ref.shape[1]
        owners = owner_ref[...]
        i, j = iota((blocks, blocks), 0), iota((blocks, blocks), 1)

        def down(value):
            return total(jnp.where(i == j, value, 0), 1)

        def across(value):
            return total(jnp.where(i == j, value, 0), 0)

        first_c = down(first)
        after_c = total(jnp.where(j == i + 1, first, 0), 1) + jnp.where(i[:, :1] == blocks - 1, rows, 0)
        after = across(after_c)
        adapter_c = total(jnp.where(iota((blocks, rows), 1) == first_c, request_ref[...], 0), 1)
        ids = iota((blocks, pool), 1)
        owner_c = total(jnp.where(ids == adapter_c, owners, 0), 1)
        slot_c = total(jnp.where((owners == owner_c) & (ids < adapter_c), 1, 0), 1)
        owner, slot = across(owner_c), across(slot_c)
        before = (owner == owner_c) & (j < i)
        turn_c = total(jnp.where(before, 1, 0), 1)
        offset_c = total(jnp.where(before, after - first, 0), 1)
        turn, offset = across(turn_c), across(offset_c)

        r, b = iota((rows, blocks), 0), iota((rows, blocks), 1)
        member = (first <= r) & (r < after)
        spot = r[:, :1] + total(jnp.where(member, offset - first, 0), 1)
        row_slot = total(jnp.where(member, slot, 0), 1)
        r_row = iota((blocks, rows), 1)
        row_owner = total(jnp.where((first_c <= r_row) & (r_row < after_c), owner_c, 0), 0)
        count = info_ref.shape[0]
        goes = jnp.where(iota((count, rows), 0) == row_owner, 1.0, 0.0).astype(jnp.bfloat16)
        asks = jnp.where(iota((rows, lanes), 1) == spot, row_slot, 0).astype(jnp.float32).astype(jnp.bfloat16)
        info = jnp.dot(goes, asks, preferred_element_type=jnp.float32)
        goes = jnp.where(iota((count, blocks), 0) == owner, 1.0, 0.0).astype(jnp.bfloat16)
        asks = jnp.where(iota((blocks, lanes), 1) == PAIR_ROWS + turn_c, slot_c, 0)
        asks = asks.astype(jnp.float32).astype(jnp.bfloat16)
        info_ref[...] = info + jnp.dot(goes, asks, preferred_element_type=jnp.float32)

        t = iota((blocks, token_count), 1)
        member = (first_c * steps <= t) & (t < after_c * steps)
        row_ref[...] = t[:1] + total(
            jnp.where(member, (owner_c * PAIR_ROWS + offset_c - first_c) * steps, 0), 0
        )
        t = iota((token_count, blocks), 0)
        member = (first * steps <= t) & (t < after * steps)
        column_ref[...] = t[:, :1] + total(
            jnp.where(member, (owner * PAIR_ROWS + offset - first) * steps, 0), 1
        )
        fetch_ref[...] = total(jnp.where(member, owner * PAIR + turn, 0), 1)

    spots = iota((here * each, token_count), 0) + pl.program_id(0) * (here * each)
    pick = jnp.where(spots == row_ref[...], 1.0, 0.0).astype(jnp.bfloat16)
    picked = jnp.dot(pick, tokens_ref[...], preferred_element_type=jnp.float32)
    for k in range(here):
        asked = info_ref[pl.ds(pl.program_id(0) * here + k, 1), :]
        parts = [picked[k * each:(k + 1) * each, c * lanes:(c + 1) * lanes] for c in range(depth // lanes)]
        parts.append(jnp.where(iota((ASK_ROWS, lanes), 0) == 0, asked, 0.0))
        sent_ref[k] = jnp.concatenate(parts, axis=0).astype(jnp.bfloat16)


def place(first, request, owners, tokens, steps, replicas):
    token_count, depth = tokens.shape
    rows = PAIR_ROWS * steps * depth // LANES + ASK_ROWS
    here = 16
    whole = lambda shape: pl.BlockSpec(shape, lambda i: (0, 0))
    return pl.pallas_call(
        functools.partial(place_kernel, steps),
        grid=(replicas // here,),
        in_specs=[
            whole((1, first.shape[0])), whole((1, request.shape[0])), whole((1, owners.shape[0])),
            whole((token_count, depth)),
        ],
        out_specs=[
            pl.BlockSpec((here, rows, LANES), lambda i: (i, 0, 0)),
            whole((token_count, 1)), whole((token_count, 1)),
        ],
        out_shape=[
            jax.ShapeDtypeStruct((replicas, rows, LANES), jnp.bfloat16),
            jax.ShapeDtypeStruct((token_count, 1), jnp.int32),
            jax.ShapeDtypeStruct((token_count, 1), jnp.int32),
        ],
        scratch_shapes=[pltpu.VMEM((1, token_count), jnp.int32), pltpu.VMEM((replicas, LANES), jnp.float32)],
        compiler_params=pltpu.CompilerParams(vmem_limit_bytes=24 * 2**20),
        name="place_rows",
    )(first[None], request[None], owners[None], tokens)


def rank_kernel(steps, rows_ref, maps_ref, ups_ref, out_ref):
    here, _, lanes = rows_ref.shape
    each = PAIR_ROWS * steps
    width = lanes // 2
    depth = maps_ref.shape[0]
    tokens, slots, picks = [], [], []
    for k in range(here):
        got = rows_ref[k].astype(jnp.float32)
        chunks = [got[c * each:(c + 1) * each] for c in range(depth // lanes)]
        tokens.append(jnp.concatenate(chunks, axis=1))
        asked = got[each * (depth // lanes):][:1]
        shape = (each, lanes)
        slots.append(total(jnp.where(iota(shape, 1) == iota(shape, 0) // steps, asked, 0.0), 1))
        shape = (PAIR * width, ups_ref.shape[0])
        i = iota((PAIR * width, 1), 0)
        turn = total(jnp.where(iota((PAIR * width, lanes), 1) == PAIR_ROWS + i // width, asked, 0.0), 1)
        at = turn.astype(jnp.int32) * width + i % width
        picks.append(jnp.where(iota(shape, 1) == at, 1.0, 0.0).astype(jnp.bfloat16))
    every = jnp.dot(
        jnp.concatenate(tokens, axis=0).astype(jnp.bfloat16), maps_ref[...], preferred_element_type=jnp.float32
    )
    slot = jnp.concatenate(slots, axis=0).astype(jnp.int32)
    two = jnp.zeros((here * each, lanes), jnp.float32)
    for pair in range(every.shape[1] // lanes):
        two = jnp.where(slot // 2 == pair, every[:, pair * lanes:(pair + 1) * lanes], two)
    own = jnp.where(slot % 2 == 1, two[:, width:], two[:, :width])
    high = own.astype(jnp.bfloat16).astype(jnp.float32)
    both = jnp.concatenate([high, own - high], axis=1)
    ups = jnp.dot(jnp.concatenate(picks, axis=0), ups_ref[...], preferred_element_type=jnp.float32)
    for k in range(here):
        out_ref[k] = jnp.concatenate(
            [
                ups[k * PAIR * width:(k + 1) * PAIR * width],
                both[k * each:(k + 1) * each],
            ],
            axis=0,
        ).astype(jnp.bfloat16)


def rank_products(rows, maps, ups, steps):
    replicas, count, lanes = rows.shape
    here = 8
    out_rows = PAIR * lanes // 2 + PAIR_ROWS * steps
    whole = lambda x: pl.BlockSpec(x.shape, lambda i: (0, 0))
    return pl.pallas_call(
        functools.partial(rank_kernel, steps),
        grid=(replicas // here,),
        in_specs=[pl.BlockSpec((here, count, lanes), lambda i: (i, 0, 0)), whole(maps), whole(ups)],
        out_specs=pl.BlockSpec((here, out_rows, lanes), lambda i: (i, 0, 0)),
        out_shape=jax.ShapeDtypeStruct((replicas, out_rows, lanes), jnp.bfloat16),
        compiler_params=pltpu.CompilerParams(vmem_limit_bytes=60 * 2**20),
        cost_estimate=pl.CostEstimate(flops=2**32, bytes_accessed=8 * 2**20, transcendentals=0),
        name="rank_products",
    )(rows, maps, ups)


def collect_kernel(column_ref, returned_ref, out_ref):
    replicas, rows, lanes = returned_ref.shape
    tokens, width = column_ref.shape[0], lanes // 2
    rows -= PAIR * width
    got = returned_ref[...].astype(jnp.float32)[:, PAIR * width:]
    got = got.reshape(replicas * rows, lanes).astype(jnp.bfloat16)
    pick = jnp.where(iota((tokens, replicas * rows), 1) == column_ref[...], 1.0, 0.0).astype(jnp.bfloat16)
    both = jnp.dot(pick, got, preferred_element_type=jnp.float32)
    value = both[:, :width] + both[:, width:]
    out_ref[...] = jnp.concatenate([value[: tokens // 2], value[tokens // 2:]], axis=1)


def collect(column, returned):
    tokens = column.shape[0]
    lanes = returned.shape[2]
    return pl.pallas_call(
        collect_kernel,
        grid=(1,),
        in_specs=[
            pl.BlockSpec((tokens, 1), lambda i: (0, 0)),
            pl.BlockSpec(returned.shape, lambda i: (0, 0, 0)),
        ],
        out_specs=pl.BlockSpec((tokens // 2, lanes), lambda i: (0, 0)),
        out_shape=jax.ShapeDtypeStruct((tokens // 2, lanes), jnp.float32),
        compiler_params=pltpu.CompilerParams(vmem_limit_bytes=24 * 2**20),
        name="collect",
    )(column, returned)


def heads_first(value, heads):
    return jnp.concatenate([value[:, h * HD:(h + 1) * HD] for h in range(heads)], axis=0)


def cached_kernel(steps, bias_ref, queries_ref, keys_ref, values_ref, mixed_ref, weight_ref):
    heads = queries_ref.shape[1] // HD
    rows = keys_ref.shape[0] // GROUP if keys_ref.ndim == 3 else 1
    cache = keys_ref.shape[1]
    count = GROUP * steps
    for g in range(rows):
        query = heads_first(queries_ref[g * count:(g + 1) * count, :], heads)
        keys = keys_ref[g * GROUP:(g + 1) * GROUP].reshape(GROUP * cache, HD)
        values = values_ref[g * GROUP:(g + 1) * GROUP].reshape(GROUP * cache, HD)
        score = lax.dot_general(query, keys, (((1,), (1,)), ((), ())), preferred_element_type=jnp.float32)
        shape = score.shape
        own = (iota(shape, 0) // steps) % GROUP == iota(shape, 1) // cache
        score = jnp.where(own, score * HD ** -0.5 + bias_ref[g], masked_score)
        highest = jnp.max(score, axis=1, keepdims=True)
        exped = jnp.exp(score - highest)
        summed = total(exped, 1)
        mixed = jnp.dot(exped.astype(jnp.bfloat16), values, preferred_element_type=jnp.float32)
        mixed_ref[g] = mixed / summed
        weight_ref[g] = jnp.broadcast_to(highest + jnp.log(summed), mixed.shape)


def cached_attention(lengths, queries, keys, values, steps):
    rows, cache = keys.shape[:2]
    heads = queries.shape[1] // HD
    groups = rows // GROUP
    count = GROUP * steps * heads
    live = jnp.arange(cache, dtype=jnp.int32)[None, :] < lengths[:, None]
    bias = jnp.where(live, 0.0, masked_score).astype(jnp.float32).reshape(groups, 1, GROUP * cache)
    per = 2
    return pl.pallas_call(
        functools.partial(cached_kernel, steps),
        grid=(groups // per,),
        in_specs=[
            pl.BlockSpec((per, 1, GROUP * cache), lambda i: (i, 0, 0)),
            pl.BlockSpec((per * GROUP * steps, heads * HD), lambda i: (i, 0)),
            pl.BlockSpec((per * GROUP, cache, HD), lambda i: (i, 0, 0)),
            pl.BlockSpec((per * GROUP, cache, HD), lambda i: (i, 0, 0)),
        ],
        out_specs=[pl.BlockSpec((per, count, HD), lambda i: (i, 0, 0))] * 2,
        out_shape=[jax.ShapeDtypeStruct((groups, count, HD), jnp.float32)] * 2,
        compiler_params=pltpu.CompilerParams(vmem_limit_bytes=24 * 2**20),
        cost_estimate=pl.CostEstimate(flops=2**31, bytes_accessed=8 * 2**20, transcendentals=2**20),
        name="cached_attention",
    )(bias, queries, keys, values)


def finish_kernel(steps, rank, fetch_ref, a_ref, b_ref, c_ref, d_ref, first_ref, second_ref, base_ref, queries_ref, mixed_ref, weight_ref, fresh_ref, out_ref, held_ref):
    heads = queries_ref.shape[1] // HD
    count = GROUP * steps
    tokens = fetch_ref.shape[0]

    @pl.when(pl.program_id(0) == 0)
    def _():
        summed = (a_ref[...] + b_ref[...]) + (c_ref[...] + d_ref[...])
        width = summed.shape[1] // 2
        low = jnp.concatenate([summed[:, :width], summed[:, width:]], axis=0)
        fetch = fetch_ref[...]
        lanes = iota((tokens, LANES), 1) // rank
        owners = first_ref.shape[0]
        for side in range(2):
            four = jnp.concatenate([low[:, side * rank:(side + 1) * rank]] * (LANES // rank), axis=1)
            delta = jnp.zeros((tokens, HD), jnp.float32)
            for turn, maps_ref in enumerate((first_ref, second_ref)):
                spread = jnp.concatenate(
                    [
                        jnp.where(fetch == PAIR * (lanes + k * (LANES // rank)) + turn, four, 0.0).astype(jnp.bfloat16)
                        for k in range(owners * rank // LANES)
                    ],
                    axis=1,
                )
                maps = maps_ref[:, side * rank:(side + 1) * rank, :].reshape(owners * rank, HD)
                delta += jnp.dot(spread, maps, preferred_element_type=jnp.float32)
            new = base_ref[:, side * HD:(side + 1) * HD] + delta
            held_ref[:, side * HD:(side + 1) * HD] = new.astype(jnp.bfloat16)
        fresh_ref[...] = held_ref[...]

    for g in range(mixed_ref.shape[0]):
        start = pl.multiple_of((pl.program_id(0) * mixed_ref.shape[0] + g) * count, count)
        new = held_ref[pl.ds(start, count), :]
        query = heads_first(queries_ref[g * count:(g + 1) * count, :], heads)
        score = lax.dot_general(
            query, new[:, :HD], (((1,), (1,)), ((), ())), preferred_element_type=jnp.float32
        )
        i, j = iota(score.shape, 0), iota(score.shape, 1)
        seen = ((i // steps) % GROUP == j // steps) & (j % steps <= i % steps)
        score = jnp.where(seen, score * HD ** -0.5, masked_score)
        weight = weight_ref[g]
        highest = jnp.maximum(jnp.max(score, axis=1, keepdims=True), weight)
        exped = jnp.exp(score - highest[:, :count]).astype(jnp.bfloat16)
        cached = jnp.exp(weight - highest)
        ones = jnp.ones((count, HD), jnp.bfloat16)
        both = jnp.dot(
            exped, jnp.concatenate([new[:, HD:], ones], axis=1), preferred_element_type=jnp.float32
        )
        mixed = (mixed_ref[g] * cached + both[:, :HD]) / (cached + both[:, HD:])
        for h in range(heads):
            part = mixed[h * count:(h + 1) * count].reshape(GROUP, steps, HD)
            out_ref[g * GROUP:(g + 1) * GROUP, :, h * HD:(h + 1) * HD] = part.astype(jnp.bfloat16)


def finish(fetch, parts, returned, base, queries, mixed, weight, steps, rank):
    tokens, features = queries.shape
    groups, rows = mixed.shape[:2]
    per = 4
    whole = lambda x: pl.BlockSpec(x.shape, lambda i: (0,) * x.ndim)
    block = pl.BlockSpec((per * GROUP * steps, features), lambda i: (i, 0))
    ups = lambda k: pl.BlockSpec((returned.shape[0], PAIR * rank, HD), lambda i: (0, k, 0))
    return pl.pallas_call(
        functools.partial(finish_kernel, steps, rank),
        grid=(groups // per,),
        in_specs=[whole(fetch)] + [whole(p) for p in parts] + [ups(0), ups(1), whole(base), block]
        + [pl.BlockSpec((per, rows, HD), lambda i: (i, 0, 0))] * 2,
        out_specs=[
            pl.BlockSpec(base.shape, lambda i: (0, 0)),
            pl.BlockSpec((per * GROUP, steps, features), lambda i: (i, 0, 0)),
        ],
        out_shape=[
            jax.ShapeDtypeStruct(base.shape, jnp.bfloat16),
            jax.ShapeDtypeStruct((tokens // steps, steps, features), jnp.bfloat16),
        ],
        scratch_shapes=[pltpu.VMEM(base.shape, jnp.bfloat16)],
        compiler_params=pltpu.CompilerParams(vmem_limit_bytes=32 * 2**20),
        name="finish",
    )(fetch, *parts, returned, returned, base, queries, mixed, weight)


def shifted(value, dx, dy):
    pairs = [(t, ((t // 2 + dx) % 4) * 2 + ((t % 2) ^ dy)) for t in range(8)]
    return lax.ppermute(value, "tensor", pairs)


def project(tokens, key_value_weight):
    half = tokens.shape[0] // 2
    here = lax.axis_index("tensor")
    x, y = here >> 1, here & 1
    depth = tokens.shape[1]

    def product(piece, dx, dy):
        start = ((((x - dx) & 3) << 1) | (y ^ dy)) * depth
        part = lax.dynamic_slice_in_dim(key_value_weight, start, depth, 0)
        return jnp.dot(piece, part.reshape(depth, -1), preferred_element_type=jnp.float32)

    right = shifted(tokens, 1, 0)
    left = shifted(tokens, -1, 0)
    across = shifted(tokens, 0, 1)
    right_across = shifted(across, 1, 0)
    left_across = shifted(across, -1, 0)
    far = jnp.concatenate([shifted(right[:half], 1, 0), shifted(left[half:], -1, 0)], axis=0)
    far_across = shifted(far, 0, 1)
    base = product(tokens, 0, 0) + product(across, 0, 1)
    base = base + product(right, 1, 0) + product(left, -1, 0)
    base = base + product(far, 2, 0)
    return base, lambda: product(right_across, 1, 1) + product(left_across, -1, 1) + product(far_across, 2, 1)


def per_device(
    hidden,
    queries,
    key_cache_rows,
    value_cache_rows,
    lengths,
    request_adapter,
    block_first_row,
    adapter_owner_group,
    key_value_weight,
    adapter_down_weight,
    adapter_up_weight,
):
    row_count, steps, depth = hidden.shape
    replicas = lax.axis_size("replica")
    token_count = row_count * steps
    held, sides, rank = adapter_down_weight.shape[:3]
    tokens = hidden.reshape(token_count, depth)

    sent, column, fetch = place(
        block_first_row, request_adapter, adapter_owner_group, tokens, steps, replicas
    )
    received = lax.all_to_all(sent, "replica", split_axis=0, concat_axis=0, tiled=True)

    near, last = project(tokens, key_value_weight)
    query_tokens = queries.reshape(token_count, -1)
    mixed, weight = cached_attention(lengths, query_tokens, key_cache_rows, value_cache_rows, steps)

    down = adapter_down_weight.reshape(held * sides * rank, depth).T
    received, near, mixed, weight, down = lax.optimization_barrier((received, near, mixed, weight, down))
    products = rank_products(
        received,
        down,
        adapter_up_weight.reshape(held * sides * rank, HD),
        steps,
    )
    returned = lax.all_to_all(products, "replica", split_axis=0, concat_axis=0, tiled=True)
    mine = collect(column, returned)
    mine = mine + shifted(mine, 0, 1)
    parts = (mine, shifted(mine, 2, 0), shifted(mine, 1, 0), shifted(mine, -1, 0))
    fresh, attended = finish(fetch, parts, returned, near + last(), query_tokens, mixed, weight, steps, rank)
    return fresh.reshape(row_count, steps, sides, HD), attended


def solution(mesh):
    placed = (
        P("replica", None, "tensor"),
        P("replica", None, "tensor"),
        P("replica", None, "tensor"),
        P("replica", None, "tensor"),
        P("replica"),
        P("replica"),
        P("replica"),
        P(),
        P(None, None, "tensor"),
        P("replica", None, None, "tensor"),
        P("replica", None, None, "tensor"),
    )
    return jax.shard_map(
        per_device,
        mesh=mesh,
        in_specs=placed,
        out_specs=(P("replica", None, None, "tensor"), P("replica", None, "tensor")),
        check_vma=False,
    )
```
